32 devices in a mesh: groups: 2 (over x), dp: 16 (over z, y, core).
Axes of the slice: x: 2, y: 2, z: 4, core: 2. Of those that a mesh axis runs over, the one named last changes fastest.
Arguments:
- tokens: bfloat16 [32768, 2048], P(('groups', 'dp')), parts along dimension 0, may hold values from -6 to 6
- legal_moves: int32 [2048, 20], P(('groups', 'dp')), parts along dimension 0, may hold values from 0 to 1, as said below
- action_label: int32 [2048], P(('groups', 'dp')), parts along dimension 0, may hold values from 0 to 19, as said below
- value_weight: bfloat16 [16384, 1024], P('dp'), may hold values from -0.125 to 0.125
- value_prior: bfloat16 [16384, 1024], P('dp'), may hold values from -0.125 to 0.125
- query_weight: bfloat16 [8, 8, 2048], replicated, may hold values from -0.125 to 0.125
- query_prior: bfloat16 [8, 8, 2048], replicated, may hold values from -0.125 to 0.125
- policy_head: float32 [8, 20, 1024], replicated, may hold values from -0.875 to 0.875
- head_prior: float32 [8, 20, 1024], replicated, may hold values from -0.875 to 0.875
Outputs:
- weight_grad: float32 [32768, 1024], P(('groups', 'dp')), parts along dimension 0
- row_loss: float32 [2048], P(('groups', 'dp')), parts along dimension 0
The draws below stay inside these ranges and needn't reach their ends.
There are 2 independent parts, one for each index of `groups`. The reference program is written for one: setup_inputs(seed, part) draws one part's arguments, and reference() takes and returns one part's arrays. A program takes and returns all parts, laid end to end along the dimension named above; an argument that names none is the same for every part. Nothing has to cross between parts.
Inputs may be any that keep to these rules, and one draw needn't show every extreme that they name: `action_label`: every row's label is one of its legal moves. `legal_moves`: every row has at least one legal move.
All inputs are finite; a program needn't handle non-finite values.
Results may differ from the reference program's by a relative error of at most 0.0071.
Values may be sent and summed in bfloat16 or wider, within the bound.
No kernel may reach another device: no remote copies, remote signals or barrier semaphores. Data moves between devices by JAX's collectives and lax.ppermute only.
A program may use at most 128 MiB of HBM per device.

```python
import jax
import jax.numpy as jnp
from jax import lax

D = 2048
H = 8
DH = 128
A = 20
OBS = 16
LEVELS = 8
ROW_DEV = 64
GROUP = 2
ROWS = 1024


def legal_pair(key):
    label_key, move_key = jax.random.split(key)
    labels = jax.random.randint(label_key, (ROWS,), 0, A, dtype=jnp.int32)
    random_moves = jax.random.randint(move_key, (ROWS, A), 0, 2, dtype=jnp.int32)
    chosen = (jnp.arange(A, dtype=jnp.int32)[None, :] == labels[:, None]).astype(jnp.int32)
    return (labels, jnp.maximum(random_moves, chosen))


def draw_legal_moves(key, part):
    labels, legal_mask = legal_pair(key)
    return legal_mask


def draw_action_label(key, part):
    labels, legal_mask = legal_pair(key)
    return labels


def levels(own_key, shape, pieces, least, high):
    loudness = 1.0
    for axis_at, parts in pieces:
        heights = jax.random.uniform(jax.random.fold_in(jax.random.fold_in(own_key, 6), axis_at), (parts,), jnp.float32, least / len(pieces), high / len(pieces))
        loudness = loudness * jnp.repeat(jnp.exp(heights), shape[axis_at] // parts).reshape((-1,) + (1,) * (len(shape) - 1 - axis_at))
    return loudness


def normal_values(own_key, dims, width, reach, cuts=(), kind=jnp.bfloat16):
    result = jax.random.normal(own_key, dims, jnp.float32) * width
    if len(cuts) > 0:
        result = levels(own_key, dims, cuts, -0.22, 0.18) * result
    return jnp.clip(result, min=-reach, max=reach).astype(kind)


def setup_inputs(seed: int = 0, part: int = 0) -> dict:
    splits = jax.random.split(jax.random.key(seed), 10)
    own_keys = jax.random.split(jax.random.fold_in(splits[9], part), 10)
    return {
        "tokens": normal_values(own_keys[0], (ROWS * OBS, D), 1.0, 6.0, ((0, 16),)),
        "legal_moves": draw_legal_moves(jax.random.fold_in(jax.random.fold_in(splits[9], part), 71), part),
        "action_label": draw_action_label(jax.random.fold_in(jax.random.fold_in(splits[9], part), 71), part),
        "value_weight": normal_values(splits[3], (LEVELS * D, H * DH), D ** -0.5, 0.125, ((0, 16),)),
        "value_prior": normal_values(splits[4], (LEVELS * D, H * DH), D ** -0.5, 0.125, ((0, 16),)),
        "query_weight": normal_values(splits[5], (LEVELS, H, D), D ** -0.5, 0.125),
        "query_prior": normal_values(splits[6], (LEVELS, H, D), D ** -0.5, 0.125),
        "policy_head": normal_values(splits[7], (LEVELS, A, H * DH), 0.15, 0.875, (), jnp.float32),
        "head_prior": normal_values(splits[8], (LEVELS, A, H * DH), 0.15, 0.875, (), jnp.float32),
    }


def policy_of(tokens, value_proj, query_proj, move_head, legal_mask):
    row_count = legal_mask.shape[0]
    scores = lax.dot_general(tokens, query_proj, (((1,), (1,)), ((), ())),
                             preferred_element_type=jnp.float32).reshape(row_count, OBS, H)
    capped = 5.0 * jnp.tanh(scores / 5.0)
    exp_scores = jnp.exp(capped)
    attention = (exp_scores / jnp.sum(exp_scores, axis=1, keepdims=True)).astype(jnp.bfloat16)
    values = jnp.dot(tokens, value_proj, preferred_element_type=jnp.float32).astype(jnp.bfloat16)
    values = values.reshape(row_count, OBS, H, DH)
    pooled = jnp.einsum("rth,rthe->rhe", attention.astype(jnp.float32), values.astype(jnp.float32),
                        precision=lax.Precision.HIGHEST).reshape(row_count, H * DH)
    raw_logits = lax.dot_general(pooled, move_head, (((1,), (1,)), ((), ())), precision=lax.Precision.HIGHEST)
    logits = 30.0 * jnp.tanh(raw_logits / 30.0)
    legal_float = legal_mask.astype(jnp.float32)
    exp_logits = jnp.exp(logits) * legal_float
    partition = jnp.sum(exp_logits, axis=1, keepdims=True)
    return logits, exp_logits / partition, logits - jnp.log(partition), attention


def reference(tokens, legal_moves, action_label, value_weight, value_prior,
              query_weight, query_prior, policy_head, head_prior):
    level_rows = ROW_DEV * GROUP
    grads = []
    losses = []
    for level_index in range(LEVELS):
        row_start = level_index * level_rows
        level_tokens = tokens[row_start * OBS:(row_start + level_rows) * OBS]
        legal_mask = legal_moves[row_start:row_start + level_rows]
        labels = action_label[row_start:row_start + level_rows]
        move_head = policy_head[level_index]
        logits, policy, log_policy, attention = policy_of(
            level_tokens, value_weight[level_index * D:(level_index + 1) * D], query_weight[level_index],
            move_head, legal_mask)
        legal_float = legal_mask.astype(jnp.float32)
        if level_index == 0:
            partner = legal_float / jnp.sum(legal_float, axis=1, keepdims=True)
        else:
            unused, partner, unused_log, unused_attention = policy_of(
                level_tokens, value_prior[(level_index - 1) * D:level_index * D], query_prior[level_index - 1],
                head_prior[level_index - 1], legal_mask)
        onehot = (labels[:, None] == jnp.arange(A, dtype=jnp.int32)[None, :]).astype(jnp.float32)
        target = 0.5 * onehot + 0.5 * partner
        losses.append(-jnp.sum(target * log_policy, axis=1))
        logit_grad = (policy - target) * (1.0 - (logits / 30.0) ** 2)
        pooled_grad = jnp.dot(logit_grad, move_head, precision=lax.Precision.HIGHEST).reshape(level_rows, 1, H, DH)
        value_grad = (attention.astype(jnp.float32)[..., None] * pooled_grad).astype(jnp.bfloat16)
        value_grad = value_grad.reshape(level_rows * OBS, H * DH)
        grads.append(jnp.dot(level_tokens.T, value_grad, preferred_element_type=jnp.float32))
    return jnp.concatenate(grads, axis=0), jnp.concatenate(losses, axis=0)
```

```python
import jax
import jax.numpy as jnp
from jax import lax
from jax.sharding import PartitionSpec as P

H = 8
DH = 128
A = 20
OBS = 16
LEVELS = 8
EXACT = lax.Precision.HIGHEST


def partner_2(block, axis, bit):
    count = lax.axis_size(axis)
    route = []
    for low in range(count):
        high = low | 1 << bit
        if high != low and high < count:
            route += [(low, high), (high, low)]
    return lax.ppermute(block, axis, route)


def shifted(block, axis, distance):
    devices = range(lax.axis_size(axis))
    route = [(i - distance, i) for i in devices if i - distance in devices]
    return lax.ppermute(block, axis, route)


def head_map(proj, move_head):
    depth = proj.shape[0]
    product = jnp.einsum(
        "dhe,ahe->had",
        proj.astype(jnp.float32).reshape(depth, H, DH),
        move_head.reshape(A, H, DH),
        precision=EXACT,
    )
    return product.reshape(H * A, depth).astype(jnp.bfloat16)


def gather_columns(block, member, bit_count):
    for bit_place in range(bit_count):
        received = partner_2(block, "dp", bit_place)
        upper_side = member // (1 << bit_place) % 2 == 1
        lower_half = jnp.where(upper_side, received, block)
        upper_half = jnp.where(upper_side, block, received)
        block = jnp.concatenate([lower_half, upper_half], axis=1)
    return block


def scatter_columns(block, member, bit_count):
    for bit_place in reversed(range(bit_count)):
        half = block.shape[1] // 2
        upper_side = member // (1 << bit_place) % 2 == 1
        kept = jnp.where(upper_side, block[:, half:], block[:, :half])
        sent = jnp.where(upper_side, block[:, :half], block[:, half:])
        block = kept + partner_2(sent, "dp", bit_place)
    return block


def attention_of(tokens, query_proj):
    scores = lax.dot_general(
        tokens, query_proj, (((1,), (1,)), ((), ())), preferred_element_type=jnp.float32
    ).reshape(-1, OBS, H)
    exp_scores = jnp.exp(5.0 * jnp.tanh(scores / 5.0))
    attention = exp_scores / jnp.sum(exp_scores, axis=1, keepdims=True)
    return attention.astype(jnp.bfloat16).astype(jnp.float32)


def policy_of(tokens, attention, mapped, legal_float):
    row_count = legal_float.shape[0]
    moved = lax.dot_general(
        tokens, mapped, (((1,), (1,)), ((), ())), preferred_element_type=jnp.float32
    ).reshape(row_count, OBS, H, A)
    raw_logits = jnp.sum(attention[..., None] * moved, axis=(1, 2))
    logits = 30.0 * jnp.tanh(raw_logits / 30.0)
    exp_logits = jnp.exp(logits) * legal_float
    partition = jnp.sum(exp_logits, axis=1, keepdims=True)
    return logits, exp_logits / partition, logits - jnp.log(partition)


def general_device(
    tokens, legal_moves, action_label, value_weight, value_prior,
    query_weight, query_prior, policy_head, head_prior,
):
    group_size = lax.axis_size("dp") // LEVELS
    bit_count = group_size.bit_length() - 1
    device_place = lax.axis_index("dp")
    level_index = device_place // group_size
    member = device_place % group_size
    lower_index = jnp.maximum(level_index - 1, 0)

    def of_level(array, index):
        return lax.dynamic_index_in_dim(array, index, 0, keepdims=False)

    move_head = of_level(policy_head, level_index)
    prior_map = head_map(value_prior, of_level(head_prior, level_index))
    own_map = head_map(value_weight, move_head)
    lower_map = gather_columns(shifted(prior_map, "dp", group_size), member, bit_count)
    own_map = gather_columns(own_map, member, bit_count)
    attention = attention_of(tokens, of_level(query_weight, level_index))
    lower_attention = attention_of(tokens, of_level(query_prior, lower_index))
    legal_float = legal_moves.astype(jnp.float32)
    logits, policy, log_policy = policy_of(tokens, attention, own_map, legal_float)
    _, lower_policy, _ = policy_of(tokens, lower_attention, lower_map, legal_float)
    uniform_policy = legal_float / jnp.sum(legal_float, axis=1, keepdims=True)
    partner = jnp.where(level_index == 0, uniform_policy, lower_policy)
    onehot = (action_label[:, None] == jnp.arange(A, dtype=jnp.int32)[None, :]).astype(jnp.float32)
    target = 0.5 * onehot + 0.5 * partner
    row_loss = -jnp.sum(target * log_policy, axis=1)
    logit_grad = (policy - target) * (1.0 - (logits / 30.0) ** 2)
    token_grad = attention[..., None] * logit_grad[:, None, None, :]
    token_grad = token_grad.astype(jnp.bfloat16).reshape(tokens.shape[0], H * A)
    mapped_grad = lax.dot_general(
        token_grad, tokens, (((0,), (0,)), ((), ())), preferred_element_type=jnp.float32
    )
    mapped_grad = scatter_columns(mapped_grad, member, bit_count).reshape(H, A, -1)
    weight_grad = jnp.einsum(
        "had,ahe->dhe", mapped_grad, move_head.reshape(A, H, DH), precision=EXACT
    )
    return weight_grad.reshape(-1, H * DH), row_loss


def solution(mesh):
    return jax.shard_map(
        general_device,
        mesh=mesh,
        in_specs=(
            P(("groups", "dp"), None),
            P(("groups", "dp"), None),
            P(("groups", "dp")),
            P("dp", None),
            P("dp", None),
            P(),
            P(),
            P(),
            P(),
        ),
        out_specs=(P(("groups", "dp"), None), P(("groups", "dp"))),
        check_vma=False,
    )
```

```python
import jax
import jax.numpy as jnp
from jax import lax
from jax.experimental import pallas as pl
from jax.experimental.pallas import tpu as pltpu
from jax.sharding import PartitionSpec as P

H = 8
DH = 128
A = 20
OBS = 16
LEVELS = 8
EXACT = lax.Precision.HIGHEST


def partner_2(block, axis, bit):
    count = lax.axis_size(axis)
    route = []
    for low in range(count):
        high = low | 1 << bit
        if high != low and high < count:
            route += [(low, high), (high, low)]
    return lax.ppermute(block, axis, route)


def shifted(block, axis, distance):
    devices = range(lax.axis_size(axis))
    route = [(i - distance, i) for i in devices if i - distance in devices]
    return lax.ppermute(block, axis, route)


def head_map(proj, move_head):
    depth = proj.shape[0]
    product = jnp.einsum(
        "dhe,ahe->had",
        proj.astype(jnp.float32).reshape(depth, H, DH),
        move_head.reshape(A, H, DH),
        precision=EXACT,
    )
    return product.reshape(H * A, depth).astype(jnp.bfloat16)


def gather_columns(block, member, bit_count):
    for bit_place in range(bit_count):
        received = partner_2(block, "dp", bit_place)
        upper_side = member // (1 << bit_place) % 2 == 1
        lower_half = jnp.where(upper_side, received, block)
        upper_half = jnp.where(upper_side, block, received)
        block = jnp.concatenate([lower_half, upper_half], axis=1)
    return block


def scatter_columns(block, member, bit_count):
    for bit_place in reversed(range(bit_count)):
        half = block.shape[1] // 2
        upper_side = member // (1 << bit_place) % 2 == 1
        kept = jnp.where(upper_side, block[:, half:], block[:, :half])
        sent = jnp.where(upper_side, block[:, :half], block[:, half:])
        block = kept + partner_2(sent, "dp", bit_place)
    return block


def attention_of(tokens, query_proj):
    scores = lax.dot_general(
        tokens, query_proj, (((1,), (1,)), ((), ())), preferred_element_type=jnp.float32
    ).reshape(-1, OBS, H)
    exp_scores = jnp.exp(5.0 * jnp.tanh(scores / 5.0))
    attention = exp_scores / jnp.sum(exp_scores, axis=1, keepdims=True)
    return attention.astype(jnp.bfloat16).astype(jnp.float32)


def policy_of(tokens, attention, mapped, legal_float):
    row_count = legal_float.shape[0]
    moved = lax.dot_general(
        tokens, mapped, (((1,), (1,)), ((), ())), preferred_element_type=jnp.float32
    ).reshape(row_count, OBS, H, A)
    raw_logits = jnp.sum(attention[..., None] * moved, axis=(1, 2))
    logits = 30.0 * jnp.tanh(raw_logits / 30.0)
    exp_logits = jnp.exp(logits) * legal_float
    partition = jnp.sum(exp_logits, axis=1, keepdims=True)
    return logits, exp_logits / partition, logits - jnp.log(partition)


def general_device(
    tokens, legal_moves, action_label, value_weight, value_prior,
    query_weight, query_prior, policy_head, head_prior,
):
    group_size = lax.axis_size("dp") // LEVELS
    bit_count = group_size.bit_length() - 1
    device_place = lax.axis_index("dp")
    level_index = device_place // group_size
    member = device_place % group_size
    lower_index = jnp.maximum(level_index - 1, 0)

    def of_level(array, index):
        return lax.dynamic_index_in_dim(array, index, 0, keepdims=False)

    move_head = of_level(policy_head, level_index)
    prior_map = head_map(value_prior, of_level(head_prior, level_index))
    own_map = head_map(value_weight, move_head)
    lower_map = gather_columns(shifted(prior_map, "dp", group_size), member, bit_count)
    own_map = gather_columns(own_map, member, bit_count)
    attention = attention_of(tokens, of_level(query_weight, level_index))
    lower_attention = attention_of(tokens, of_level(query_prior, lower_index))
    legal_float = legal_moves.astype(jnp.float32)
    logits, policy, log_policy = policy_of(tokens, attention, own_map, legal_float)
    _, lower_policy, _ = policy_of(tokens, lower_attention, lower_map, legal_float)
    uniform_policy = legal_float / jnp.sum(legal_float, axis=1, keepdims=True)
    partner = jnp.where(level_index == 0, uniform_policy, lower_policy)
    onehot = (action_label[:, None] == jnp.arange(A, dtype=jnp.int32)[None, :]).astype(jnp.float32)
    target = 0.5 * onehot + 0.5 * partner
    row_loss = -jnp.sum(target * log_policy, axis=1)
    logit_grad = (policy - target) * (1.0 - (logits / 30.0) ** 2)
    token_grad = attention[..., None] * logit_grad[:, None, None, :]
    token_grad = token_grad.astype(jnp.bfloat16).reshape(tokens.shape[0], H * A)
    mapped_grad = lax.dot_general(
        token_grad, tokens, (((0,), (0,)), ((), ())), preferred_element_type=jnp.float32
    )
    mapped_grad = scatter_columns(mapped_grad, member, bit_count).reshape(H, A, -1)
    weight_grad = jnp.einsum(
        "had,ahe->dhe", mapped_grad, move_head.reshape(A, H, DH), precision=EXACT
    )
    return weight_grad.reshape(-1, H * DH), row_loss


PAIR = 2
TOP = 16
SPREAD = H * A
BLOCK_ROWS = 16
F32 = jnp.float32
BF16 = jnp.bfloat16
VMEM_BYTES = 48 * 2**20


def dot_nt(left, right):
    return lax.dot_general(left, right, (((1,), (1,)), ((), ())), preferred_element_type=F32)


def dot_nn(left, right):
    return lax.dot_general(left, right, (((1,), (0,)), ((), ())), preferred_element_type=F32)


def dot_tn(left, right, precision=None):
    return lax.dot_general(
        left, right, (((0,), (0,)), ((), ())), preferred_element_type=F32, precision=precision
    )


def split_high(value):
    high = value.astype(BF16)
    return high, (value - high.astype(F32)).astype(BF16)


def spread_heads(rows):
    width = rows.shape[1]
    top = rows[:TOP]
    lane_head = lax.broadcasted_iota(jnp.int32, (TOP, width), 1) // DH
    pieces = [jnp.where(lane_head == h, top, 0.0) for h in range(H)]
    rest = rows[TOP:A]
    rest = jnp.concatenate([rest, rest], axis=0)
    lane_head = lax.broadcasted_iota(jnp.int32, (8, width), 1) // DH
    upper = lax.broadcasted_iota(jnp.int32, (8, width), 0) // 4
    pieces += [jnp.where(lane_head == 2 * i + upper, rest, 0.0) for i in range(H // 2)]
    return jnp.concatenate(pieces, axis=0)


def level_here(group_size):
    return lax.axis_index("dp") // group_size


def build_spread(level, head_ref, spread_ref):
    rows = head_ref[:, pl.ds(level, 1), :].reshape(A, H * DH)
    high, low = split_high(spread_heads(rows))
    spread_ref[:SPREAD, :] = high
    spread_ref[SPREAD:, :] = low


def folded(spread_ref, proj):
    product = dot_nt(spread_ref[...], proj)
    return product[:SPREAD] + product[SPREAD:]


def map_kernel(level_ref, head_ref, proj_ref, out_ref, spread_ref):
    @pl.when(pl.program_id(0) == 0)
    def _():
        build_spread(level_ref[0], head_ref, spread_ref)

    out_ref[...] = folded(spread_ref, proj_ref[...]).astype(BF16)


def prior_map_of(level, head_t, proj, chunk):
    depth, width = proj.shape
    return pl.pallas_call(
        map_kernel,
        grid_spec=pltpu.PrefetchScalarGridSpec(
            num_scalar_prefetch=1,
            grid=(depth // chunk,),
            in_specs=[
                pl.BlockSpec(head_t.shape, lambda i, s: (0, 0, 0)),
                pl.BlockSpec((chunk, width), lambda i, s: (i, 0)),
            ],
            out_specs=pl.BlockSpec((SPREAD, chunk), lambda i, s: (0, i)),
            scratch_shapes=[pltpu.VMEM((2 * SPREAD, width), BF16)],
        ),
        out_shape=jax.ShapeDtypeStruct((SPREAD, depth), BF16),
        compiler_params=pltpu.CompilerParams(vmem_limit_bytes=VMEM_BYTES),
        cost_estimate=pl.CostEstimate(
            flops=4 * SPREAD * depth * width, bytes_accessed=2 * depth * width, transcendentals=0
        ),
    )(level, head_t, proj)


def pool_kernel(place_ref, tokens_ref, query_ref, prior_ref, out_ref):
    block = tokens_ref.shape[0]
    half = out_ref.shape[3]
    level = place_ref[0]
    lower = jnp.maximum(level - 1, 0)
    tokens = tokens_ref[...]
    scores = jnp.concatenate(
        [dot_nt(query_ref[level], tokens), dot_nt(prior_ref[lower], tokens)], axis=0
    )
    exp_scores = jnp.exp(5.0 * jnp.tanh(scores / 5.0))
    first, rest = split_high(exp_scores)
    second, third = split_high(exp_scores - first.astype(F32))
    row_of = lax.broadcasted_iota(jnp.int32, (block, block), 0) // OBS
    column_of = lax.broadcasted_iota(jnp.int32, (block, block), 1) // OBS
    same_row = (row_of == column_of).astype(F32).astype(BF16)
    parts = dot_nn(jnp.concatenate([first, second, third], axis=0), same_row)
    total = parts[: 2 * H] + parts[2 * H : 4 * H] + parts[4 * H :]
    attention = (exp_scores / total).astype(BF16).astype(F32)
    mask = (
        lax.broadcasted_iota(jnp.int32, (BLOCK_ROWS, block), 0)
        == lax.broadcasted_iota(jnp.int32, (BLOCK_ROWS, block), 1) // OBS
    )
    spread = jnp.concatenate(
        [jnp.where(mask, attention[i : i + 1], 0.0) for i in range(2 * H)], axis=0
    ).astype(BF16)
    start = pl.multiple_of(place_ref[1] * half, half)
    pooled = dot_nn(spread, tokens_ref[:, pl.ds(start, half)])
    out_ref[...] = pooled.astype(BF16).reshape(2, H, BLOCK_ROWS, half)


def pooled_tokens(place, tokens, query_weight, query_prior):
    count, depth = tokens.shape
    half = depth // PAIR
    block = BLOCK_ROWS * OBS
    return pl.pallas_call(
        pool_kernel,
        grid_spec=pltpu.PrefetchScalarGridSpec(
            num_scalar_prefetch=1,
            grid=(count // block,),
            in_specs=[
                pl.BlockSpec((block, depth), lambda i, s: (i, 0)),
                pl.BlockSpec(query_weight.shape, lambda i, s: (0, 0, 0)),
                pl.BlockSpec(query_prior.shape, lambda i, s: (0, 0, 0)),
            ],
            out_specs=pl.BlockSpec((2, H, BLOCK_ROWS, half), lambda i, s: (0, 0, i, 0)),
        ),
        out_shape=jax.ShapeDtypeStruct((2, H, count // OBS, half), BF16),
        compiler_params=pltpu.CompilerParams(vmem_limit_bytes=VMEM_BYTES),
        cost_estimate=pl.CostEstimate(
            flops=2 * count * depth * 2 * H + 4 * count * H * BLOCK_ROWS * half,
            bytes_accessed=2 * count * depth + 2 * count * half,
            transcendentals=4 * count * H,
        ),
    )(place, tokens, query_weight, query_prior)


def finish_raw(top, rest):
    rest = rest[:8] + rest[8:]
    rest = rest + jnp.concatenate([rest[4:], rest[:4]], axis=0)
    return jnp.concatenate([top, rest], axis=0)


def raw_sums(tables, own_ref, peer_ref):
    rows = 2 * own_ref.shape[2]
    top = jnp.zeros((TOP, rows), F32)
    rest = jnp.zeros((TOP, rows), F32)
    place = lax.broadcasted_iota(jnp.int32, (TOP, rows), 0) // 4
    for h in range(H):
        left = []
        for table in tables:
            left += [table[h * TOP : (h + 1) * TOP], table[H * TOP + h // 4 * TOP :][:TOP]]
        pooled = jnp.concatenate([own_ref[0, h], peer_ref[0, h]], axis=0)
        result = dot_nt(jnp.concatenate(left, axis=0), pooled)
        for i in range(len(tables)):
            top = top + result[2 * i * TOP :][:TOP]
            rest = rest + jnp.where(place == h % 4, result[(2 * i + 1) * TOP :][:TOP], 0.0)
    return top, rest


def own_kernel(level_ref, head_ref, proj_ref, own_ref, peer_ref, out_ref, spread_ref, sum_ref):
    step = pl.program_id(0)

    @pl.when(step == 0)
    def _():
        build_spread(level_ref[0], head_ref, spread_ref)
        sum_ref[...] = jnp.zeros_like(sum_ref)

    tables = split_high(folded(spread_ref, proj_ref[...]))
    top, rest = raw_sums(tables, own_ref, peer_ref)
    sum_ref[:TOP] += top
    sum_ref[TOP:] += rest

    @pl.when(step == pl.num_programs(0) - 1)
    def _():
        out_ref[...] = finish_raw(sum_ref[:TOP], sum_ref[TOP:])


def own_raw(level, head_t, proj, own_pool, peer_pool, chunk):
    depth, width = proj.shape
    rows = own_pool.shape[2]
    pool_spec = pl.BlockSpec((1, H, rows, chunk), lambda i, s: (0, 0, 0, i))
    return pl.pallas_call(
        own_kernel,
        grid_spec=pltpu.PrefetchScalarGridSpec(
            num_scalar_prefetch=1,
            grid=(depth // chunk,),
            in_specs=[
                pl.BlockSpec(head_t.shape, lambda i, s: (0, 0, 0)),
                pl.BlockSpec((chunk, width), lambda i, s: (i, 0)),
                pool_spec,
                pool_spec,
            ],
            out_specs=pl.BlockSpec((24, 2 * rows), lambda i, s: (0, 0)),
            scratch_shapes=[
                pltpu.VMEM((2 * SPREAD, width), BF16),
                pltpu.VMEM((2 * TOP, 2 * rows), F32),
            ],
        ),
        out_shape=jax.ShapeDtypeStruct((24, 2 * rows), F32),
        compiler_params=pltpu.CompilerParams(vmem_limit_bytes=VMEM_BYTES),
        cost_estimate=pl.CostEstimate(
            flops=4 * SPREAD * depth * width, bytes_accessed=4 * depth * width, transcendentals=0
        ),
    )(level, head_t, proj, own_pool, peer_pool)


def lower_kernel(table_ref, own_ref, peer_ref, raw_ref, legal_ref, label_ref, out_ref):
    rows = own_ref.shape[2]
    out_ref[:24] = raw_ref[...]
    top, rest = raw_sums([table_ref[...]], own_ref, peer_ref)
    out_ref[24:48] = finish_raw(top, rest)
    out_ref[48:72] = jnp.zeros((24, 2 * rows), F32)
    out_ref[48 : 48 + A, :rows] = legal_ref[...].astype(F32)
    out_ref[48 + A : 49 + A, :rows] = label_ref[...].astype(F32)


def lower_raw(table, own_pool, peer_pool, raw, legal_t, label):
    _, _, rows, half = own_pool.shape
    pool_spec = pl.BlockSpec((1, H, rows, half), lambda i: (1, 0, 0, 0))

    def whole(array):
        return pl.BlockSpec(array.shape, lambda i: (0, 0))

    return pl.pallas_call(
        lower_kernel,
        grid=(1,),
        in_specs=[whole(table), pool_spec, pool_spec, whole(raw), whole(legal_t), whole(label)],
        out_specs=pl.BlockSpec((72, 2 * rows), lambda i: (0, 0)),
        out_shape=jax.ShapeDtypeStruct((72, 2 * rows), F32),
        compiler_params=pltpu.CompilerParams(vmem_limit_bytes=VMEM_BYTES),
        cost_estimate=pl.CostEstimate(
            flops=8 * TOP * rows * H * half, bytes_accessed=4 * rows * H * half, transcendentals=0
        ),
    )(table, own_pool, peer_pool, raw, legal_t, label)


def policy_rows(raw, legal):
    logits = 30.0 * jnp.tanh(raw / 30.0)
    exp_logits = jnp.exp(logits) * legal
    partition = jnp.sum(exp_logits, axis=0, keepdims=True)
    return logits, exp_logits / partition, logits - jnp.log(partition)


def grad_kernel(level_ref, mine_ref, theirs_ref, head_ref, own_ref, peer_ref, out_ref, loss_ref, diag_ref):
    rows = own_ref.shape[2]

    @pl.when(pl.program_id(0) == 0)
    def _():
        level = level_ref[0]
        theirs = theirs_ref[:48]
        theirs = jnp.concatenate([theirs[:, rows:], theirs[:, :rows]], axis=1)
        raw = mine_ref[:48] + theirs
        told = jnp.concatenate([mine_ref[48:72, :rows], theirs_ref[48:72, :rows]], axis=1)
        move = lax.broadcasted_iota(jnp.int32, told.shape, 0)
        legal = jnp.where(move < A, told, 0.0)
        onehot = (move.astype(F32) == told[A : A + 1]).astype(F32)
        logits, policy, log_policy = policy_rows(raw[:24], legal)
        _, lower_policy, _ = policy_rows(raw[24:], legal)
        uniform = legal / jnp.sum(legal, axis=0, keepdims=True)
        partner = jnp.where(level == 0, uniform, lower_policy)
        target = 0.5 * onehot + 0.5 * partner
        loss = -jnp.sum(target * log_policy, axis=0, keepdims=True)
        loss_ref[...] = loss[:, :rows]
        logit_grad = (policy - target) * (1.0 - (logits / 30.0) ** 2)
        head = head_ref[:, pl.ds(level, 1), :].reshape(A, H * DH)
        head = jnp.concatenate([head, jnp.zeros((24 - A, H * DH), F32)], axis=0)
        pooled_grad = dot_tn(logit_grad, head, lax.Precision.HIGHEST).astype(BF16)
        diag_ref[...] = jnp.zeros_like(diag_ref)
        for h in range(H):
            at = h % 2
            diag_ref[h // 2, at * 2 * rows : (at + 1) * 2 * rows, at * DH : (at + 1) * DH] = (
                pooled_grad[:, h * DH : (h + 1) * DH]
            )

    for pair in range(H // 2):
        pooled = jnp.concatenate(
            [own_ref[0, 2 * pair], peer_ref[0, 2 * pair], own_ref[0, 2 * pair + 1], peer_ref[0, 2 * pair + 1]],
            axis=0,
        )
        out_ref[:, pair * 2 * DH : (pair + 1) * 2 * DH] = dot_tn(pooled, diag_ref[pair])


def gradient(level, mine, theirs, head_t, own_pool, peer_pool, chunk):
    _, _, rows, half = own_pool.shape
    width = H * DH
    pool_spec = pl.BlockSpec((1, H, rows, chunk), lambda i, s: (0, 0, 0, i))
    return pl.pallas_call(
        grad_kernel,
        grid_spec=pltpu.PrefetchScalarGridSpec(
            num_scalar_prefetch=1,
            grid=(half // chunk,),
            in_specs=[
                pl.BlockSpec(mine.shape, lambda i, s: (0, 0)),
                pl.BlockSpec(theirs.shape, lambda i, s: (0, 0)),
                pl.BlockSpec(head_t.shape, lambda i, s: (0, 0, 0)),
                pool_spec,
                pool_spec,
            ],
            out_specs=[
                pl.BlockSpec((chunk, width), lambda i, s: (i, 0)),
                pl.BlockSpec((1, rows), lambda i, s: (0, 0)),
            ],
            scratch_shapes=[pltpu.VMEM((H // 2, 4 * rows, 2 * DH), BF16)],
        ),
        out_shape=[
            jax.ShapeDtypeStruct((half, width), F32),
            jax.ShapeDtypeStruct((1, rows), F32),
        ],
        compiler_params=pltpu.CompilerParams(vmem_limit_bytes=VMEM_BYTES),
        cost_estimate=pl.CostEstimate(
            flops=8 * rows * half * width // 2,
            bytes_accessed=4 * half * width + 4 * rows * H * half,
            transcendentals=0,
        ),
    )(level, mine, theirs, head_t, own_pool, peer_pool)


def paired_device(
    tokens, legal_moves, action_label, value_weight, value_prior,
    query_weight, query_prior, policy_head, head_prior,
):
    device_place = lax.axis_index("dp")
    place = jnp.stack([device_place // PAIR, device_place % PAIR]).astype(jnp.int32)
    peer_tokens = partner_2(tokens, "dp", 0)
    head_t = jnp.transpose(policy_head, (1, 0, 2))
    prior_t = jnp.transpose(head_prior, (1, 0, 2))
    prior_map = prior_map_of(place, prior_t, value_prior, 256)
    lower_map = shifted(prior_map, "dp", PAIR)
    own_pool = pooled_tokens(place, tokens, query_weight, query_prior)
    peer_pool = pooled_tokens(place, peer_tokens, query_weight, query_prior)
    raw = own_raw(place, head_t, value_weight, own_pool, peer_pool, 256)
    mine = lower_raw(
        lower_map, own_pool, peer_pool, raw, legal_moves.T, action_label.reshape(1, -1)
    )
    theirs = partner_2(mine, "dp", 0)
    weight_grad, row_loss = gradient(place, mine, theirs, head_t, own_pool, peer_pool, 256)
    return weight_grad, row_loss.reshape(-1)


def solution(mesh):
    paired = mesh.shape["dp"] == LEVELS * PAIR
    return jax.shard_map(
        paired_device if paired else general_device,
        mesh=mesh,
        in_specs=(
            P(("groups", "dp"), None),
            P(("groups", "dp"), None),
            P(("groups", "dp")),
            P("dp", None),
            P("dp", None),
            P(),
            P(),
            P(),
            P(),
        ),
        out_specs=(P(("groups", "dp"), None), P(("groups", "dp"))),
        check_vma=False,
    )
```

```python
import jax
import jax.numpy as jnp
from jax import lax
from jax.experimental import pallas as pl
from jax.experimental.pallas import tpu as pltpu
from jax.sharding import PartitionSpec as P

H = 8
DH = 128
A = 20
OBS = 16
LEVELS = 8
EXACT = lax.Precision.HIGHEST


def partner_2(block, axis, bit):
    count = lax.axis_size(axis)
    route = []
    for low in range(count):
        high = low | 1 << bit
        if high != low and high < count:
            route += [(low, high), (high, low)]
    return lax.ppermute(block, axis, route)


def shifted(block, axis, distance):
    devices = range(lax.axis_size(axis))
    route = [(i - distance, i) for i in devices if i - distance in devices]
    return lax.ppermute(block, axis, route)


def head_map(proj, move_head):
    depth = proj.shape[0]
    product = jnp.einsum(
        "dhe,ahe->had",
        proj.astype(jnp.float32).reshape(depth, H, DH),
        move_head.reshape(A, H, DH),
        precision=EXACT,
    )
    return product.reshape(H * A, depth).astype(jnp.bfloat16)


def gather_columns(block, member, bit_count):
    for bit_place in range(bit_count):
        received = partner_2(block, "dp", bit_place)
        upper_side = member // (1 << bit_place) % 2 == 1
        lower_half = jnp.where(upper_side, received, block)
        upper_half = jnp.where(upper_side, block, received)
        block = jnp.concatenate([lower_half, upper_half], axis=1)
    return block


def scatter_columns(block, member, bit_count):
    for bit_place in reversed(range(bit_count)):
        half = block.shape[1] // 2
        upper_side = member // (1 << bit_place) % 2 == 1
        kept = jnp.where(upper_side, block[:, half:], block[:, :half])
        sent = jnp.where(upper_side, block[:, :half], block[:, half:])
        block = kept + partner_2(sent, "dp", bit_place)
    return block


def attention_of(tokens, query_proj):
    scores = lax.dot_general(
        tokens, query_proj, (((1,), (1,)), ((), ())), preferred_element_type=jnp.float32
    ).reshape(-1, OBS, H)
    exp_scores = jnp.exp(5.0 * jnp.tanh(scores / 5.0))
    attention = exp_scores / jnp.sum(exp_scores, axis=1, keepdims=True)
    return attention.astype(jnp.bfloat16).astype(jnp.float32)


def policy_of(tokens, attention, mapped, legal_float):
    row_count = legal_float.shape[0]
    moved = lax.dot_general(
        tokens, mapped, (((1,), (1,)), ((), ())), preferred_element_type=jnp.float32
    ).reshape(row_count, OBS, H, A)
    raw_logits = jnp.sum(attention[..., None] * moved, axis=(1, 2))
    logits = 30.0 * jnp.tanh(raw_logits / 30.0)
    exp_logits = jnp.exp(logits) * legal_float
    partition = jnp.sum(exp_logits, axis=1, keepdims=True)
    return logits, exp_logits / partition, logits - jnp.log(partition)


def general_device(
    tokens, legal_moves, action_label, value_weight, value_prior,
    query_weight, query_prior, policy_head, head_prior,
):
    group_size = lax.axis_size("dp") // LEVELS
    bit_count = group_size.bit_length() - 1
    device_place = lax.axis_index("dp")
    level_index = device_place // group_size
    member = device_place % group_size
    lower_index = jnp.maximum(level_index - 1, 0)

    def of_level(array, index):
        return lax.dynamic_index_in_dim(array, index, 0, keepdims=False)

    move_head = of_level(policy_head, level_index)
    prior_map = head_map(value_prior, of_level(head_prior, level_index))
    own_map = head_map(value_weight, move_head)
    lower_map = gather_columns(shifted(prior_map, "dp", group_size), member, bit_count)
    own_map = gather_columns(own_map, member, bit_count)
    attention = attention_of(tokens, of_level(query_weight, level_index))
    lower_attention = attention_of(tokens, of_level(query_prior, lower_index))
    legal_float = legal_moves.astype(jnp.float32)
    logits, policy, log_policy = policy_of(tokens, attention, own_map, legal_float)
    _, lower_policy, _ = policy_of(tokens, lower_attention, lower_map, legal_float)
    uniform_policy = legal_float / jnp.sum(legal_float, axis=1, keepdims=True)
    partner = jnp.where(level_index == 0, uniform_policy, lower_policy)
    onehot = (action_label[:, None] == jnp.arange(A, dtype=jnp.int32)[None, :]).astype(jnp.float32)
    target = 0.5 * onehot + 0.5 * partner
    row_loss = -jnp.sum(target * log_policy, axis=1)
    logit_grad = (policy - target) * (1.0 - (logits / 30.0) ** 2)
    token_grad = attention[..., None] * logit_grad[:, None, None, :]
    token_grad = token_grad.astype(jnp.bfloat16).reshape(tokens.shape[0], H * A)
    mapped_grad = lax.dot_general(
        token_grad, tokens, (((0,), (0,)), ((), ())), preferred_element_type=jnp.float32
    )
    mapped_grad = scatter_columns(mapped_grad, member, bit_count).reshape(H, A, -1)
    weight_grad = jnp.einsum(
        "had,ahe->dhe", mapped_grad, move_head.reshape(A, H, DH), precision=EXACT
    )
    return weight_grad.reshape(-1, H * DH), row_loss


PAIR = 2
TOP = 16
SPREAD = H * A
BLOCK_ROWS = 16
F32 = jnp.float32
BF16 = jnp.bfloat16
PAD = 24
CHUNKS = 4
GRAD_CHUNKS = 4
DH_BITS = 7
OBS_BITS = 4
MIB = 2**20
PRIOR_MIB = 54
OWN_MIB = 48
PEER_MIB = 40


def dot_nt(left, right):
    return lax.dot_general(left, right, (((1,), (1,)), ((), ())), preferred_element_type=F32)


def dot_nn(left, right):
    return lax.dot_general(left, right, (((1,), (0,)), ((), ())), preferred_element_type=F32)


def dot_tn(left, right):
    return lax.dot_general(
        left, right, (((0,), (0,)), ((), ())), preferred_element_type=F32
    )


def split_high(value):
    high = value.astype(BF16)
    return high, (value - high.astype(F32)).astype(BF16)


def spread_heads(rows):
    width = rows.shape[1]
    top = rows[:TOP]
    lane_head = lax.broadcasted_iota(jnp.int32, (TOP, width), 1) >> DH_BITS
    pieces = [jnp.where(lane_head == h, top, 0.0) for h in range(H)]
    rest = rows[TOP:A]
    rest = jnp.concatenate([rest, rest], axis=0)
    lane_head = lax.broadcasted_iota(jnp.int32, (8, width), 1) >> DH_BITS
    upper = lax.broadcasted_iota(jnp.int32, (8, width), 0) >> 2
    pieces += [jnp.where(lane_head == 2 * i + upper, rest, 0.0) for i in range(H // 2)]
    return jnp.concatenate(pieces, axis=0)


def chunk_copies(source_ref, target_ref, sems, first):
    chunk = source_ref.shape[0] // CHUNKS
    copies = []
    for i in range(CHUNKS):
        rows = pl.ds(i * chunk, chunk)
        copies.append(
            pltpu.make_async_copy(source_ref.at[rows], target_ref.at[rows], sems.at[first + i])
        )
    return copies


def spread_into(spread_ref, head_buf, level):
    head = head_buf[:, pl.ds(level, 1), :].reshape(A, H * DH)
    high, low = split_high(spread_heads(head))
    spread_ref[:SPREAD, :] = high
    spread_ref[SPREAD:, :] = low
    return head


def fold_into(out_ref, proj_buf, spread_ref, parts):
    product = dot_nt(spread_ref[...], proj_buf[...])
    product = product[:SPREAD] + product[SPREAD:]
    if parts == 1:
        out_ref[...] = product.astype(BF16)
    else:
        high, low = split_high(product)
        out_ref[:SPREAD] = high
        out_ref[SPREAD:] = low


def prior_kernel(head_ref, proj_ref, out_ref, head_buf, proj_buf, spread_ref, sems):
    head_copy = pltpu.make_async_copy(head_ref, head_buf, sems.at[CHUNKS])
    head_copy.start()
    copies = chunk_copies(proj_ref, proj_buf, sems, 0)
    for copy in copies:
        copy.start()
    head_copy.wait()
    spread_into(spread_ref, head_buf, lax.axis_index("dp") // PAIR)
    for copy in copies:
        copy.wait()
    fold_into(out_ref, proj_buf, spread_ref, 1)


IN_HBM = pl.BlockSpec(memory_space=pltpu.HBM)
IN_VMEM = pl.BlockSpec(memory_space=pltpu.VMEM)


def prior_fold(head_t, proj):
    depth, width = proj.shape
    return pl.pallas_call(
        prior_kernel,
        in_specs=[IN_HBM, IN_HBM],
        out_specs=IN_VMEM,
        out_shape=jax.ShapeDtypeStruct((SPREAD, depth), BF16),
        scratch_shapes=[
            pltpu.VMEM(head_t.shape, F32),
            pltpu.VMEM(proj.shape, BF16),
            pltpu.VMEM((2 * SPREAD, width), BF16),
            pltpu.SemaphoreType.DMA((CHUNKS + 1,)),
        ],
        compiler_params=pltpu.CompilerParams(vmem_limit_bytes=PRIOR_MIB * MIB),
        cost_estimate=pl.CostEstimate(
            flops=4 * SPREAD * depth * width, bytes_accessed=2 * depth * width, transcendentals=0
        ),
    )(head_t, proj)


def pool_into(out_ref, tokens_ref, copies, query_ref, prior_ref):
    count = tokens_ref.shape[0]
    half = out_ref.shape[3]
    block = BLOCK_ROWS * OBS
    blocks = count // block
    device_place = lax.axis_index("dp")
    level = device_place // PAIR
    lower = jnp.maximum(level - 1, 0)
    queries = jnp.concatenate(
        [query_ref[level].astype(F32), prior_ref[lower].astype(F32)], axis=0
    ).astype(BF16)
    row_of = lax.broadcasted_iota(jnp.int32, (block, block), 0) >> OBS_BITS
    column_of = lax.broadcasted_iota(jnp.int32, (block, block), 1) >> OBS_BITS
    same_row = (row_of == column_of).astype(F32).astype(BF16)
    mask = (
        lax.broadcasted_iota(jnp.int32, (BLOCK_ROWS, block), 0)
        == lax.broadcasted_iota(jnp.int32, (BLOCK_ROWS, block), 1) >> OBS_BITS
    )
    start = pl.multiple_of(device_place % PAIR * half, half)
    scores = []
    for step in range(blocks // 2):
        for copy in copies[2 * step : 2 * step + 2]:
            copy.wait()
        two = dot_nt(queries, tokens_ref[2 * step * block : 2 * (step + 1) * block])
        scores += [two[:, :block], two[:, block:]]
    exp_scores = jnp.exp(5.0 * jnp.tanh(jnp.concatenate(scores, axis=0) / 5.0))
    first, rest = split_high(exp_scores)
    second, third = split_high(exp_scores - first.astype(F32))
    parts = dot_nn(jnp.concatenate([first, second, third], axis=0), same_row)
    rows = 2 * H * blocks
    total = parts[:rows] + parts[rows : 2 * rows] + parts[2 * rows :]
    attention = (exp_scores / total).astype(BF16).astype(F32)
    for i in range(blocks):
        at = 2 * H * i
        spread = jnp.concatenate(
            [jnp.where(mask, attention[at + j : at + j + 1], 0.0) for j in range(2 * H)], axis=0
        ).astype(BF16)
        pooled = dot_nn(spread, tokens_ref[i * block : (i + 1) * block, pl.ds(start, half)])
        out_ref[:, :, i * BLOCK_ROWS : (i + 1) * BLOCK_ROWS, :] = pooled.astype(BF16).reshape(
            2, H, BLOCK_ROWS, half
        )


def own_kernel(
    tokens_ref, query_ref, prior_ref, head_ref, proj_ref,
    pool_ref, map_ref, wide_ref, tokens_buf, head_buf, proj_buf, spread_ref, sems,
):
    token_copies = chunk_copies(tokens_ref, tokens_buf, sems, 0)
    proj_copies = chunk_copies(proj_ref, proj_buf, sems, CHUNKS)
    head_copy = pltpu.make_async_copy(head_ref, head_buf, sems.at[2 * CHUNKS])
    for copy in [head_copy] + proj_copies + token_copies:
        copy.start()
    head_copy.wait()
    head = spread_into(spread_ref, head_buf, lax.axis_index("dp") // PAIR)
    for copy in proj_copies:
        copy.wait()
    fold_into(map_ref, proj_buf, spread_ref, 2)
    head = jnp.concatenate([head, jnp.zeros((PAD - A, H * DH), F32)], axis=0)
    lane_head = lax.broadcasted_iota(jnp.int32, (PAD, H * DH), 1) >> DH_BITS
    wide = [jnp.where(lane_head == h, head, 0.0) for h in range(H)]
    wide_ref[...] = jnp.concatenate(wide, axis=0).astype(BF16)
    pool_into(pool_ref, tokens_buf, token_copies, query_ref, prior_ref)


def own_side(tokens, query_weight, query_prior, head_t, proj):
    count, width = tokens.shape
    half = proj.shape[0]
    return pl.pallas_call(
        own_kernel,
        in_specs=[IN_HBM, IN_VMEM, IN_VMEM, IN_HBM, IN_HBM],
        out_specs=[IN_VMEM] * 3,
        out_shape=[
            jax.ShapeDtypeStruct((2, H, count // OBS, half), BF16),
            jax.ShapeDtypeStruct((2 * SPREAD, half), BF16),
            jax.ShapeDtypeStruct((H * PAD, H * DH), BF16),
        ],
        scratch_shapes=[
            pltpu.VMEM(tokens.shape, BF16),
            pltpu.VMEM(head_t.shape, F32),
            pltpu.VMEM(proj.shape, BF16),
            pltpu.VMEM((2 * SPREAD, H * DH), BF16),
            pltpu.SemaphoreType.DMA((2 * CHUNKS + 1,)),
        ],
        compiler_params=pltpu.CompilerParams(vmem_limit_bytes=OWN_MIB * MIB),
        cost_estimate=pl.CostEstimate(
            flops=2 * count * width * 2 * H + 4 * count * H * BLOCK_ROWS * half,
            bytes_accessed=4 * count * width,
            transcendentals=4 * count * H,
        ),
    )(tokens, query_weight, query_prior, head_t, proj)


def peer_kernel(
    tokens_ref, query_ref, prior_ref, map_ref, own_ref, pool_ref, raw_ref, tokens_buf, sems
):
    copies = chunk_copies(tokens_ref, tokens_buf, sems, 0)
    for copy in copies:
        copy.start()
    tables = [map_ref[:SPREAD], map_ref[SPREAD:]]
    own_raw = raw_sums(tables, [own_ref], 0)
    pool_into(pool_ref, tokens_buf, copies, query_ref, prior_ref)
    raw_ref[...] = jnp.concatenate([own_raw, raw_sums(tables, [pool_ref], 0)], axis=1)


def peer_side(tokens, query_weight, query_prior, own_map, own_pool):
    count, width = tokens.shape
    half = own_map.shape[1]
    return pl.pallas_call(
        peer_kernel,
        in_specs=[IN_HBM, IN_VMEM, IN_VMEM, IN_VMEM, IN_VMEM],
        out_specs=[IN_VMEM] * 2,
        out_shape=[
            jax.ShapeDtypeStruct((2, H, count // OBS, half), BF16),
            jax.ShapeDtypeStruct((PAD, 2 * count // OBS), F32),
        ],
        scratch_shapes=[pltpu.VMEM(tokens.shape, BF16), pltpu.SemaphoreType.DMA((CHUNKS,))],
        compiler_params=pltpu.CompilerParams(vmem_limit_bytes=PEER_MIB * MIB),
        cost_estimate=pl.CostEstimate(
            flops=2 * count * width * 2 * H + 4 * count * H * BLOCK_ROWS * half,
            bytes_accessed=2 * count * width + 2 * count * half,
            transcendentals=4 * count * H,
        ),
    )(tokens, query_weight, query_prior, own_map, own_pool)


def finish_raw(top, rest):
    rest = rest[:8] + rest[8:]
    rest = rest + jnp.concatenate([rest[4:], rest[:4]], axis=0)
    return jnp.concatenate([top, rest], axis=0)


def raw_sums(tables, pools, which):
    rows = len(pools) * pools[0].shape[2]
    top = jnp.zeros((TOP, rows), F32)
    rest = jnp.zeros((TOP, rows), F32)
    place = lax.broadcasted_iota(jnp.int32, (TOP, rows), 0) >> 2
    for h in range(H):
        left = []
        for table in tables:
            left += [table[h * TOP : (h + 1) * TOP], table[H * TOP + h // 4 * TOP :][:TOP]]
        pooled = jnp.concatenate([pool[which, h] for pool in pools], axis=0)
        result = dot_nt(jnp.concatenate(left, axis=0), pooled)
        for i in range(len(tables)):
            top = top + result[2 * i * TOP :][:TOP]
            rest = rest + jnp.where(place == h % 4, result[(2 * i + 1) * TOP :][:TOP], 0.0)
    return finish_raw(top, rest)


def lower_raw_kernel(map_ref, own_ref, peer_ref, raw_ref, legal_ref, label_ref, out_ref):
    rows = own_ref.shape[2]
    out_ref[:PAD] = raw_ref[...]
    out_ref[PAD : 2 * PAD] = raw_sums([map_ref[...]], [own_ref, peer_ref], 1)
    out_ref[2 * PAD :] = jnp.zeros((PAD, 2 * rows), F32)
    out_ref[2 * PAD : 2 * PAD + A, :rows] = legal_ref[...].astype(F32)
    out_ref[2 * PAD + A : 2 * PAD + A + 1, :rows] = label_ref[...].astype(F32)


def raw_call(kernel, rows_out, *operands):
    _, _, rows, half = operands[1].shape
    return pl.pallas_call(
        kernel,
        in_specs=[IN_VMEM] * len(operands),
        out_specs=IN_VMEM,
        out_shape=jax.ShapeDtypeStruct((rows_out, 2 * rows), F32),
        compiler_params=pltpu.CompilerParams(vmem_limit_bytes=12 * 2**20),
        cost_estimate=pl.CostEstimate(
            flops=8 * TOP * rows * H * half, bytes_accessed=4 * rows * H * half, transcendentals=0
        ),
    )(*operands)


def policy_rows(raw, legal):
    logits = 30.0 * jnp.tanh(raw / 30.0)
    exp_logits = jnp.exp(logits) * legal
    partition = jnp.sum(exp_logits, axis=0, keepdims=True)
    return logits, exp_logits / partition, logits - jnp.log(partition)


def grad_kernel(
    mine_ref, theirs_ref, wide_ref, own_ref, peer_ref, out_ref, loss_ref, out_buf, sems,
):
    rows = own_ref.shape[2]
    theirs = theirs_ref[: 2 * PAD]
    theirs = jnp.concatenate([theirs[:, rows:], theirs[:, :rows]], axis=1)
    raw = mine_ref[: 2 * PAD] + theirs
    told = jnp.concatenate([mine_ref[2 * PAD :, :rows], theirs_ref[2 * PAD :, :rows]], axis=1)
    move = lax.broadcasted_iota(jnp.int32, told.shape, 0)
    legal = jnp.where(move < A, told, 0.0)
    onehot = (move.astype(F32) == told[A : A + 1]).astype(F32)
    logits, policy, log_policy = policy_rows(raw[:PAD], legal)
    _, lower_policy, _ = policy_rows(raw[PAD:], legal)
    uniform = legal / jnp.sum(legal, axis=0, keepdims=True)
    partner = jnp.where(lax.axis_index("dp") // PAIR == 0, uniform, lower_policy)
    target = 0.5 * onehot + 0.5 * partner
    loss = -jnp.sum(target * log_policy, axis=0, keepdims=True)
    loss_ref[...] = loss[:, :rows]
    logit_grad = (policy - target) * (1.0 - (logits / 30.0) ** 2)
    high, low = split_high(logit_grad)
    left = jnp.concatenate([high.astype(F32), low.astype(F32)], axis=0).astype(BF16)
    chunk = out_buf.shape[0] // GRAD_CHUNKS
    copies = []
    for i in range(GRAD_CHUNKS):
        columns = slice(i * chunk, (i + 1) * chunk)
        narrow = []
        for h in range(H):
            pooled = jnp.concatenate([own_ref[0, h, :, columns], peer_ref[0, h, :, columns]], axis=0)
            product = dot_nn(left, pooled)
            narrow.append(product[:PAD] + product[PAD:])
        narrow = jnp.concatenate(narrow, axis=0).astype(BF16)
        out_buf[columns, :] = dot_tn(narrow, wide_ref[...])
        part = pl.ds(i * chunk, chunk)
        copies.append(pltpu.make_async_copy(out_buf.at[part], out_ref.at[part], sems.at[i]))
        copies[i].start()
    for copy in copies:
        copy.wait()


def gradient(mine, theirs, wide, own_pool, peer_pool):
    _, _, rows, half = own_pool.shape
    width = H * DH
    return pl.pallas_call(
        grad_kernel,
        in_specs=[IN_VMEM] * 5,
        out_specs=[IN_HBM, IN_VMEM],
        out_shape=[
            jax.ShapeDtypeStruct((half, width), F32),
            jax.ShapeDtypeStruct((1, rows), F32),
        ],
        scratch_shapes=[
            pltpu.VMEM((half, width), F32),
            pltpu.SemaphoreType.DMA((GRAD_CHUNKS,)),
        ],
        compiler_params=pltpu.CompilerParams(vmem_limit_bytes=16 * MIB),
        cost_estimate=pl.CostEstimate(
            flops=2 * H * PAD * half * width,
            bytes_accessed=4 * half * width + 4 * rows * H * half,
            transcendentals=0,
        ),
    )(mine, theirs, wide, own_pool, peer_pool)


def paired_device(
    tokens, legal_moves, action_label, value_weight, value_prior,
    query_weight, query_prior, policy_head, head_prior,
):
    peer_tokens = partner_2(tokens, "dp", 0)
    prior_map = prior_fold(jnp.transpose(head_prior, (1, 0, 2)), value_prior)
    lower_map = shifted(prior_map, "dp", PAIR)
    own_pool, own_map, wide = own_side(
        tokens, query_weight, query_prior, jnp.transpose(policy_head, (1, 0, 2)), value_weight
    )
    peer_pool, raw = peer_side(peer_tokens, query_weight, query_prior, own_map, own_pool)
    mine = raw_call(
        lower_raw_kernel, 3 * PAD,
        lower_map, own_pool, peer_pool, raw, legal_moves.T, action_label.reshape(1, -1),
    )
    theirs = partner_2(mine, "dp", 0)
    weight_grad, row_loss = gradient(mine, theirs, wide, own_pool, peer_pool)
    return weight_grad, row_loss.reshape(-1)


def solution(mesh):
    paired = mesh.shape["dp"] == LEVELS * PAIR
    return jax.shard_map(
        paired_device if paired else general_device,
        mesh=mesh,
        in_specs=(
            P(("groups", "dp"), None),
            P(("groups", "dp"), None),
            P(("groups", "dp")),
            P("dp", None),
            P("dp", None),
            P(),
            P(),
            P(),
            P(),
        ),
        out_specs=(P(("groups", "dp"), None), P(("groups", "dp"))),
        check_vma=False,
    )
```

```python
import jax
import jax.numpy as jnp
from jax import lax
from jax.experimental import pallas as pl
from jax.experimental.pallas import tpu as pltpu
from jax.sharding import PartitionSpec as P

H = 8
DH = 128
A = 20
OBS = 16
LEVELS = 8
EXACT = lax.Precision.HIGHEST


def partner_2(block, axis, bit):
    count = lax.axis_size(axis)
    route = []
    for low in range(count):
        high = low | 1 << bit
        if high != low and high < count:
            route += [(low, high), (high, low)]
    return lax.ppermute(block, axis, route)


def shifted(block, axis, distance):
    devices = range(lax.axis_size(axis))
    route = [(i - distance, i) for i in devices if i - distance in devices]
    return lax.ppermute(block, axis, route)


def head_map(proj, move_head):
    depth = proj.shape[0]
    product = jnp.einsum(
        "dhe,ahe->had",
        proj.astype(jnp.float32).reshape(depth, H, DH),
        move_head.reshape(A, H, DH),
        precision=EXACT,
    )
    return product.reshape(H * A, depth).astype(jnp.bfloat16)


def gather_columns(block, member, bit_count):
    for bit_place in range(bit_count):
        received = partner_2(block, "dp", bit_place)
        upper_side = member // (1 << bit_place) % 2 == 1
        lower_half = jnp.where(upper_side, received, block)
        upper_half = jnp.where(upper_side, block, received)
        block = jnp.concatenate([lower_half, upper_half], axis=1)
    return block


def scatter_columns(block, member, bit_count):
    for bit_place in reversed(range(bit_count)):
        half = block.shape[1] // 2
        upper_side = member // (1 << bit_place) % 2 == 1
        kept = jnp.where(upper_side, block[:, half:], block[:, :half])
        sent = jnp.where(upper_side, block[:, :half], block[:, half:])
        block = kept + partner_2(sent, "dp", bit_place)
    return block


def attention_of(tokens, query_proj):
    scores = lax.dot_general(
        tokens, query_proj, (((1,), (1,)), ((), ())), preferred_element_type=jnp.float32
    ).reshape(-1, OBS, H)
    exp_scores = jnp.exp(5.0 * jnp.tanh(scores / 5.0))
    attention = exp_scores / jnp.sum(exp_scores, axis=1, keepdims=True)
    return attention.astype(jnp.bfloat16).astype(jnp.float32)


def policy_of(tokens, attention, mapped, legal_float):
    row_count = legal_float.shape[0]
    moved = lax.dot_general(
        tokens, mapped, (((1,), (1,)), ((), ())), preferred_element_type=jnp.float32
    ).reshape(row_count, OBS, H, A)
    raw_logits = jnp.sum(attention[..., None] * moved, axis=(1, 2))
    logits = 30.0 * jnp.tanh(raw_logits / 30.0)
    exp_logits = jnp.exp(logits) * legal_float
    partition = jnp.sum(exp_logits, axis=1, keepdims=True)
    return logits, exp_logits / partition, logits - jnp.log(partition)


def general_device(
    tokens, legal_moves, action_label, value_weight, value_prior,
    query_weight, query_prior, policy_head, head_prior,
):
    group_size = lax.axis_size("dp") // LEVELS
    bit_count = group_size.bit_length() - 1
    device_place = lax.axis_index("dp")
    level_index = device_place // group_size
    member = device_place % group_size
    lower_index = jnp.maximum(level_index - 1, 0)

    def of_level(array, index):
        return lax.dynamic_index_in_dim(array, index, 0, keepdims=False)

    move_head = of_level(policy_head, level_index)
    prior_map = head_map(value_prior, of_level(head_prior, level_index))
    own_map = head_map(value_weight, move_head)
    lower_map = gather_columns(shifted(prior_map, "dp", group_size), member, bit_count)
    own_map = gather_columns(own_map, member, bit_count)
    attention = attention_of(tokens, of_level(query_weight, level_index))
    lower_attention = attention_of(tokens, of_level(query_prior, lower_index))
    legal_float = legal_moves.astype(jnp.float32)
    logits, policy, log_policy = policy_of(tokens, attention, own_map, legal_float)
    _, lower_policy, _ = policy_of(tokens, lower_attention, lower_map, legal_float)
    uniform_policy = legal_float / jnp.sum(legal_float, axis=1, keepdims=True)
    partner = jnp.where(level_index == 0, uniform_policy, lower_policy)
    onehot = (action_label[:, None] == jnp.arange(A, dtype=jnp.int32)[None, :]).astype(jnp.float32)
    target = 0.5 * onehot + 0.5 * partner
    row_loss = -jnp.sum(target * log_policy, axis=1)
    logit_grad = (policy - target) * (1.0 - (logits / 30.0) ** 2)
    token_grad = attention[..., None] * logit_grad[:, None, None, :]
    token_grad = token_grad.astype(jnp.bfloat16).reshape(tokens.shape[0], H * A)
    mapped_grad = lax.dot_general(
        token_grad, tokens, (((0,), (0,)), ((), ())), preferred_element_type=jnp.float32
    )
    mapped_grad = scatter_columns(mapped_grad, member, bit_count).reshape(H, A, -1)
    weight_grad = jnp.einsum(
        "had,ahe->dhe", mapped_grad, move_head.reshape(A, H, DH), precision=EXACT
    )
    return weight_grad.reshape(-1, H * DH), row_loss


PAIR = 2
TOP = 16
SPREAD = H * A
BLOCK_ROWS = 16
F32 = jnp.float32
BF16 = jnp.bfloat16
PAD = 24
GRAD_CHUNKS = 4
DH_BITS = 7
OBS_BITS = 4
MIB = 2**20
PRIOR_MIB = 12
OWN_MIB = 16
PEER_MIB = 16
PRIOR_COST = 40
SPREAD_COST = 100000
SPREAD_MIB = 53


def dot_nt(left, right):
    return lax.dot_general(left, right, (((1,), (1,)), ((), ())), preferred_element_type=F32)


def dot_nn(left, right):
    return lax.dot_general(left, right, (((1,), (0,)), ((), ())), preferred_element_type=F32)


def dot_tn(left, right):
    return lax.dot_general(
        left, right, (((0,), (0,)), ((), ())), preferred_element_type=F32
    )


def split_high(value):
    high = value.astype(BF16)
    return high, (value - high.astype(F32)).astype(BF16)


def spread_heads(rows):
    width = rows.shape[1]
    top = rows[:TOP]
    lane_head = lax.broadcasted_iota(jnp.int32, (TOP, width), 1) >> DH_BITS
    pieces = [jnp.where(lane_head == h, top, 0.0) for h in range(H)]
    rest = rows[TOP:A]
    rest = jnp.concatenate([rest, rest], axis=0)
    lane_head = lax.broadcasted_iota(jnp.int32, (8, width), 1) >> DH_BITS
    upper = lax.broadcasted_iota(jnp.int32, (8, width), 0) >> 2
    pieces += [jnp.where(lane_head == 2 * i + upper, rest, 0.0) for i in range(H // 2)]
    return jnp.concatenate(pieces, axis=0)


def spread_into(spread_ref, head_ref):
    level = lax.axis_index("dp") // PAIR
    head = head_ref[:, pl.ds(level, 1), :].reshape(A, H * DH)
    high, low = split_high(spread_heads(head))
    spread_ref[:SPREAD, :] = high
    spread_ref[SPREAD:, :] = low
    return head


def fold_into(out_ref, proj_ref, spread_ref, parts):
    product = dot_nt(spread_ref[...], proj_ref[...])
    product = product[:SPREAD] + product[SPREAD:]
    if parts == 1:
        out_ref[...] = product.astype(BF16)
    else:
        high, low = split_high(product)
        out_ref[:SPREAD] = high
        out_ref[SPREAD:] = low


def spread_kernel(head_ref, spread_ref, head_buf, sem):
    copy = pltpu.make_async_copy(head_ref, head_buf, sem)
    copy.start()
    copy.wait()
    spread_into(spread_ref, head_buf)


def prior_kernel(spread_ref, proj_ref, out_ref):
    fold_into(out_ref, proj_ref, spread_ref, 1)


IN_HBM = pl.BlockSpec(memory_space=pltpu.HBM)
IN_VMEM = pl.BlockSpec(memory_space=pltpu.VMEM)


def head_spread(head_t):
    width = head_t.shape[2]
    return pl.pallas_call(
        spread_kernel,
        in_specs=[IN_HBM],
        out_specs=IN_VMEM,
        out_shape=jax.ShapeDtypeStruct((2 * SPREAD, width), BF16),
        scratch_shapes=[pltpu.VMEM(head_t.shape, F32), pltpu.SemaphoreType.DMA],
        compiler_params=pltpu.CompilerParams(vmem_limit_bytes=SPREAD_MIB * MIB),
        cost_estimate=pl.CostEstimate(
            flops=SPREAD_COST * SPREAD * width, bytes_accessed=4 * head_t.size, transcendentals=0
        ),
    )(head_t)


def prior_fold(spread, proj):
    depth, width = proj.shape
    return pl.pallas_call(
        prior_kernel,
        in_specs=[IN_VMEM, IN_VMEM],
        out_specs=IN_VMEM,
        out_shape=jax.ShapeDtypeStruct((SPREAD, depth), BF16),
        compiler_params=pltpu.CompilerParams(vmem_limit_bytes=PRIOR_MIB * MIB),
        cost_estimate=pl.CostEstimate(
            flops=PRIOR_COST * SPREAD * depth * width,
            bytes_accessed=2 * depth * width,
            transcendentals=0,
        ),
    )(spread, proj)


def pool_into(out_ref, tokens_ref, query_ref, prior_ref):
    count = tokens_ref.shape[0]
    half = out_ref.shape[3]
    block = BLOCK_ROWS * OBS
    blocks = count // block
    device_place = lax.axis_index("dp")
    level = device_place // PAIR
    lower = jnp.maximum(level - 1, 0)
    queries = jnp.concatenate(
        [query_ref[level].astype(F32), prior_ref[lower].astype(F32)], axis=0
    ).astype(BF16)
    row_of = lax.broadcasted_iota(jnp.int32, (block, block), 0) >> OBS_BITS
    column_of = lax.broadcasted_iota(jnp.int32, (block, block), 1) >> OBS_BITS
    same_row = (row_of == column_of).astype(F32).astype(BF16)
    mask = (
        lax.broadcasted_iota(jnp.int32, (BLOCK_ROWS, block), 0)
        == lax.broadcasted_iota(jnp.int32, (BLOCK_ROWS, block), 1) >> OBS_BITS
    )
    start = pl.multiple_of(device_place % PAIR * half, half)
    scores = dot_nt(queries, tokens_ref[...])
    scores = [scores[:, i * block : (i + 1) * block] for i in range(blocks)]
    exp_scores = jnp.exp(5.0 * jnp.tanh(jnp.concatenate(scores, axis=0) / 5.0))
    first, rest = split_high(exp_scores)
    second, third = split_high(exp_scores - first.astype(F32))
    parts = dot_nn(jnp.concatenate([first, second, third], axis=0), same_row)
    rows = 2 * H * blocks
    total = parts[:rows] + parts[rows : 2 * rows] + parts[2 * rows :]
    attention = (exp_scores / total).astype(BF16).astype(F32)
    for i in range(blocks):
        at = 2 * H * i
        spread = jnp.concatenate(
            [jnp.where(mask, attention[at + j : at + j + 1], 0.0) for j in range(2 * H)], axis=0
        ).astype(BF16)
        pooled = dot_nn(spread, tokens_ref[i * block : (i + 1) * block, pl.ds(start, half)])
        out_ref[:, :, i * BLOCK_ROWS : (i + 1) * BLOCK_ROWS, :] = pooled.astype(BF16).reshape(
            2, H, BLOCK_ROWS, half
        )


def own_kernel(
    tokens_ref, query_ref, prior_ref, head_ref, proj_ref, pool_ref, map_ref, wide_ref, spread_ref
):
    head = spread_into(spread_ref, head_ref)
    fold_into(map_ref, proj_ref, spread_ref, 2)
    head = jnp.concatenate([head, jnp.zeros((PAD - A, H * DH), F32)], axis=0)
    lane_head = lax.broadcasted_iota(jnp.int32, (PAD, H * DH), 1) >> DH_BITS
    wide = [jnp.where(lane_head == h, head, 0.0) for h in range(H)]
    wide_ref[...] = jnp.concatenate(wide, axis=0).astype(BF16)
    pool_into(pool_ref, tokens_ref, query_ref, prior_ref)


def own_side(tokens, query_weight, query_prior, head_t, proj):
    count, width = tokens.shape
    half = proj.shape[0]
    return pl.pallas_call(
        own_kernel,
        in_specs=[IN_VMEM] * 5,
        out_specs=[IN_VMEM] * 3,
        out_shape=[
            jax.ShapeDtypeStruct((2, H, count // OBS, half), BF16),
            jax.ShapeDtypeStruct((2 * SPREAD, half), BF16),
            jax.ShapeDtypeStruct((H * PAD, H * DH), BF16),
        ],
        scratch_shapes=[pltpu.VMEM((2 * SPREAD, H * DH), BF16)],
        compiler_params=pltpu.CompilerParams(vmem_limit_bytes=OWN_MIB * MIB),
        cost_estimate=pl.CostEstimate(
            flops=2 * count * width * 2 * H + 4 * count * H * BLOCK_ROWS * half,
            bytes_accessed=4 * count * width,
            transcendentals=4 * count * H,
        ),
    )(tokens, query_weight, query_prior, head_t, proj)


def peer_kernel(tokens_ref, query_ref, prior_ref, map_ref, own_ref, pool_ref, raw_ref):
    pool_into(pool_ref, tokens_ref, query_ref, prior_ref)
    tables = [map_ref[:SPREAD], map_ref[SPREAD:]]
    raw_ref[...] = raw_sums(tables, [own_ref, pool_ref], 0)


def peer_side(tokens, query_weight, query_prior, own_map, own_pool):
    count, width = tokens.shape
    half = own_map.shape[1]
    return pl.pallas_call(
        peer_kernel,
        in_specs=[IN_VMEM] * 5,
        out_specs=[IN_VMEM] * 2,
        out_shape=[
            jax.ShapeDtypeStruct((2, H, count // OBS, half), BF16),
            jax.ShapeDtypeStruct((PAD, 2 * count // OBS), F32),
        ],
        compiler_params=pltpu.CompilerParams(vmem_limit_bytes=PEER_MIB * MIB),
        cost_estimate=pl.CostEstimate(
            flops=2 * count * width * 2 * H + 4 * count * H * BLOCK_ROWS * half,
            bytes_accessed=2 * count * width + 2 * count * half,
            transcendentals=4 * count * H,
        ),
    )(tokens, query_weight, query_prior, own_map, own_pool)


def finish_raw(top, rest):
    rest = rest[:8] + rest[8:]
    rest = rest + jnp.concatenate([rest[4:], rest[:4]], axis=0)
    return jnp.concatenate([top, rest], axis=0)


def raw_sums(tables, pools, which):
    rows = len(pools) * pools[0].shape[2]
    top = jnp.zeros((TOP, rows), F32)
    rest = jnp.zeros((TOP, rows), F32)
    place = lax.broadcasted_iota(jnp.int32, (TOP, rows), 0) >> 2
    for h in range(H):
        left = []
        for table in tables:
            left += [table[h * TOP : (h + 1) * TOP], table[H * TOP + h // 4 * TOP :][:TOP]]
        pooled = jnp.concatenate([pool[which, h] for pool in pools], axis=0)
        result = dot_nt(jnp.concatenate(left, axis=0), pooled)
        for i in range(len(tables)):
            top = top + result[2 * i * TOP :][:TOP]
            rest = rest + jnp.where(place == h % 4, result[(2 * i + 1) * TOP :][:TOP], 0.0)
    return finish_raw(top, rest)


def lower_raw_kernel(map_ref, own_ref, peer_ref, raw_ref, legal_ref, label_ref, out_ref):
    rows = own_ref.shape[2]
    out_ref[:PAD] = raw_ref[...]
    out_ref[PAD : 2 * PAD] = raw_sums([map_ref[...]], [own_ref, peer_ref], 1)
    out_ref[2 * PAD :] = jnp.zeros((PAD, 2 * rows), F32)
    out_ref[2 * PAD : 2 * PAD + A, :rows] = legal_ref[...].astype(F32)
    out_ref[2 * PAD + A : 2 * PAD + A + 1, :rows] = label_ref[...].astype(F32)


def raw_call(kernel, rows_out, *operands):
    _, _, rows, half = operands[1].shape
    return pl.pallas_call(
        kernel,
        in_specs=[IN_VMEM] * len(operands),
        out_specs=IN_VMEM,
        out_shape=jax.ShapeDtypeStruct((rows_out, 2 * rows), F32),
        compiler_params=pltpu.CompilerParams(vmem_limit_bytes=12 * 2**20),
        cost_estimate=pl.CostEstimate(
            flops=8 * TOP * rows * H * half, bytes_accessed=4 * rows * H * half, transcendentals=0
        ),
    )(*operands)


def policy_rows(raw, legal):
    logits = 30.0 * jnp.tanh(raw / 30.0)
    exp_logits = jnp.exp(logits) * legal
    partition = jnp.sum(exp_logits, axis=0, keepdims=True)
    return logits, exp_logits / partition, logits - jnp.log(partition)


def grad_kernel(
    mine_ref, theirs_ref, wide_ref, own_ref, peer_ref, out_ref, loss_ref, out_buf, sems,
):
    rows = own_ref.shape[2]
    theirs = theirs_ref[: 2 * PAD]
    theirs = jnp.concatenate([theirs[:, rows:], theirs[:, :rows]], axis=1)
    raw = mine_ref[: 2 * PAD] + theirs
    told = jnp.concatenate([mine_ref[2 * PAD :, :rows], theirs_ref[2 * PAD :, :rows]], axis=1)
    move = lax.broadcasted_iota(jnp.int32, told.shape, 0)
    legal = jnp.where(move < A, told, 0.0)
    onehot = (move.astype(F32) == told[A : A + 1]).astype(F32)
    logits, policy, log_policy = policy_rows(raw[:PAD], legal)
    _, lower_policy, _ = policy_rows(raw[PAD:], legal)
    uniform = legal / jnp.sum(legal, axis=0, keepdims=True)
    partner = jnp.where(lax.axis_index("dp") // PAIR == 0, uniform, lower_policy)
    target = 0.5 * onehot + 0.5 * partner
    loss = -jnp.sum(target * log_policy, axis=0, keepdims=True)
    loss_ref[...] = loss[:, :rows]
    logit_grad = (policy - target) * (1.0 - (logits / 30.0) ** 2)
    high, low = split_high(logit_grad)
    left = jnp.concatenate([high.astype(F32), low.astype(F32)], axis=0).astype(BF16)
    chunk = out_buf.shape[0] // GRAD_CHUNKS
    copies = []
    for i in range(GRAD_CHUNKS):
        columns = slice(i * chunk, (i + 1) * chunk)
        narrow = []
        for h in range(H):
            pooled = jnp.concatenate([own_ref[0, h, :, columns], peer_ref[0, h, :, columns]], axis=0)
            product = dot_nn(left, pooled)
            narrow.append(product[:PAD] + product[PAD:])
        narrow = jnp.concatenate(narrow, axis=0).astype(BF16)
        out_buf[columns, :] = dot_tn(narrow, wide_ref[...])
        part = pl.ds(i * chunk, chunk)
        copies.append(pltpu.make_async_copy(out_buf.at[part], out_ref.at[part], sems.at[i]))
        copies[i].start()
    for copy in copies:
        copy.wait()


def gradient(mine, theirs, wide, own_pool, peer_pool):
    _, _, rows, half = own_pool.shape
    width = H * DH
    return pl.pallas_call(
        grad_kernel,
        in_specs=[IN_VMEM] * 5,
        out_specs=[IN_HBM, IN_VMEM],
        out_shape=[
            jax.ShapeDtypeStruct((half, width), F32),
            jax.ShapeDtypeStruct((1, rows), F32),
        ],
        scratch_shapes=[
            pltpu.VMEM((half, width), F32),
            pltpu.SemaphoreType.DMA((GRAD_CHUNKS,)),
        ],
        compiler_params=pltpu.CompilerParams(vmem_limit_bytes=16 * MIB),
        cost_estimate=pl.CostEstimate(
            flops=2 * H * PAD * half * width,
            bytes_accessed=4 * half * width + 4 * rows * H * half,
            transcendentals=0,
        ),
    )(mine, theirs, wide, own_pool, peer_pool)


def paired_device(
    tokens, legal_moves, action_label, value_weight, value_prior,
    query_weight, query_prior, policy_head, head_prior,
):
    peer_tokens = partner_2(tokens, "dp", 0)
    spread = head_spread(jnp.transpose(head_prior, (1, 0, 2)))
    prior_map = prior_fold(spread, value_prior)
    lower_map = shifted(prior_map, "dp", PAIR)
    own_pool, own_map, wide = own_side(
        tokens, query_weight, query_prior, jnp.transpose(policy_head, (1, 0, 2)), value_weight
    )
    peer_pool, raw = peer_side(peer_tokens, query_weight, query_prior, own_map, own_pool)
    mine = raw_call(
        lower_raw_kernel, 3 * PAD,
        lower_map, own_pool, peer_pool, raw, legal_moves.T, action_label.reshape(1, -1),
    )
    theirs = partner_2(mine, "dp", 0)
    weight_grad, row_loss = gradient(mine, theirs, wide, own_pool, peer_pool)
    return weight_grad, row_loss.reshape(-1)


def solution(mesh):
    paired = mesh.shape["dp"] == LEVELS * PAIR
    return jax.shard_map(
        paired_device if paired else general_device,
        mesh=mesh,
        in_specs=(
            P(("groups", "dp"), None),
            P(("groups", "dp"), None),
            P(("groups", "dp")),
            P("dp", None),
            P("dp", None),
            P(),
            P(),
            P(),
            P(),
        ),
        out_specs=(P(("groups", "dp"), None), P(("groups", "dp"))),
        check_vma=False,
    )
```

```python
import jax
import jax.numpy as jnp
from jax import lax
from jax.experimental import pallas as pl
from jax.experimental.pallas import tpu as pltpu
from jax.sharding import PartitionSpec as P

H = 8
DH = 128
A = 20
OBS = 16
LEVELS = 8
EXACT = lax.Precision.HIGHEST


def partner_2(block, axis, bit):
    count = lax.axis_size(axis)
    route = []
    for low in range(count):
        high = low | 1 << bit
        if high != low and high < count:
            route += [(low, high), (high, low)]
    return lax.ppermute(block, axis, route)


def shifted(block, axis, distance):
    devices = range(lax.axis_size(axis))
    route = [(i - distance, i) for i in devices if i - distance in devices]
    return lax.ppermute(block, axis, route)


def head_map(proj, move_head):
    depth = proj.shape[0]
    product = jnp.einsum(
        "dhe,ahe->had",
        proj.astype(jnp.float32).reshape(depth, H, DH),
        move_head.reshape(A, H, DH),
        precision=EXACT,
    )
    return product.reshape(H * A, depth).astype(jnp.bfloat16)


def gather_columns(block, member, bit_count):
    for bit_place in range(bit_count):
        received = partner_2(block, "dp", bit_place)
        upper_side = member // (1 << bit_place) % 2 == 1
        lower_half = jnp.where(upper_side, received, block)
        upper_half = jnp.where(upper_side, block, received)
        block = jnp.concatenate([lower_half, upper_half], axis=1)
    return block


def scatter_columns(block, member, bit_count):
    for bit_place in reversed(range(bit_count)):
        half = block.shape[1] // 2
        upper_side = member // (1 << bit_place) % 2 == 1
        kept = jnp.where(upper_side, block[:, half:], block[:, :half])
        sent = jnp.where(upper_side, block[:, :half], block[:, half:])
        block = kept + partner_2(sent, "dp", bit_place)
    return block


def attention_of(tokens, query_proj):
    scores = lax.dot_general(
        tokens, query_proj, (((1,), (1,)), ((), ())), preferred_element_type=jnp.float32
    ).reshape(-1, OBS, H)
    exp_scores = jnp.exp(5.0 * jnp.tanh(scores / 5.0))
    attention = exp_scores / jnp.sum(exp_scores, axis=1, keepdims=True)
    return attention.astype(jnp.bfloat16).astype(jnp.float32)


def policy_of(tokens, attention, mapped, legal_float):
    row_count = legal_float.shape[0]
    moved = lax.dot_general(
        tokens, mapped, (((1,), (1,)), ((), ())), preferred_element_type=jnp.float32
    ).reshape(row_count, OBS, H, A)
    raw_logits = jnp.sum(attention[..., None] * moved, axis=(1, 2))
    logits = 30.0 * jnp.tanh(raw_logits / 30.0)
    exp_logits = jnp.exp(logits) * legal_float
    partition = jnp.sum(exp_logits, axis=1, keepdims=True)
    return logits, exp_logits / partition, logits - jnp.log(partition)


def general_device(
    tokens, legal_moves, action_label, value_weight, value_prior,
    query_weight, query_prior, policy_head, head_prior,
):
    group_size = lax.axis_size("dp") // LEVELS
    bit_count = group_size.bit_length() - 1
    device_place = lax.axis_index("dp")
    level_index = device_place // group_size
    member = device_place % group_size
    lower_index = jnp.maximum(level_index - 1, 0)

    def of_level(array, index):
        return lax.dynamic_index_in_dim(array, index, 0, keepdims=False)

    move_head = of_level(policy_head, level_index)
    prior_map = head_map(value_prior, of_level(head_prior, level_index))
    own_map = head_map(value_weight, move_head)
    lower_map = gather_columns(shifted(prior_map, "dp", group_size), member, bit_count)
    own_map = gather_columns(own_map, member, bit_count)
    attention = attention_of(tokens, of_level(query_weight, level_index))
    lower_attention = attention_of(tokens, of_level(query_prior, lower_index))
    legal_float = legal_moves.astype(jnp.float32)
    logits, policy, log_policy = policy_of(tokens, attention, own_map, legal_float)
    _, lower_policy, _ = policy_of(tokens, lower_attention, lower_map, legal_float)
    uniform_policy = legal_float / jnp.sum(legal_float, axis=1, keepdims=True)
    partner = jnp.where(level_index == 0, uniform_policy, lower_policy)
    onehot = (action_label[:, None] == jnp.arange(A, dtype=jnp.int32)[None, :]).astype(jnp.float32)
    target = 0.5 * onehot + 0.5 * partner
    row_loss = -jnp.sum(target * log_policy, axis=1)
    logit_grad = (policy - target) * (1.0 - (logits / 30.0) ** 2)
    token_grad = attention[..., None] * logit_grad[:, None, None, :]
    token_grad = token_grad.astype(jnp.bfloat16).reshape(tokens.shape[0], H * A)
    mapped_grad = lax.dot_general(
        token_grad, tokens, (((0,), (0,)), ((), ())), preferred_element_type=jnp.float32
    )
    mapped_grad = scatter_columns(mapped_grad, member, bit_count).reshape(H, A, -1)
    weight_grad = jnp.einsum(
        "had,ahe->dhe", mapped_grad, move_head.reshape(A, H, DH), precision=EXACT
    )
    return weight_grad.reshape(-1, H * DH), row_loss


PAIR = 2
TOP = 16
SPREAD = H * A
BLOCK_ROWS = 16
F32 = jnp.float32
BF16 = jnp.bfloat16
PAD = 24
GRAD_CHUNKS = 4
DH_BITS = 7
OBS_BITS = 4
MIB = 2**20
PRIOR_MIB = 12
OWN_MIB = 16
PEER_MIB = 16
PRIOR_COST = 40
SPREAD_COST = 100000
SPREAD_MIB = 53


def dot_nt(left, right):
    return lax.dot_general(left, right, (((1,), (1,)), ((), ())), preferred_element_type=F32)


def dot_nn(left, right):
    return lax.dot_general(left, right, (((1,), (0,)), ((), ())), preferred_element_type=F32)


def dot_tn(left, right):
    return lax.dot_general(
        left, right, (((0,), (0,)), ((), ())), preferred_element_type=F32
    )


def split_high(value):
    high = value.astype(BF16)
    return high, (value - high.astype(F32)).astype(BF16)


def spread_heads(rows):
    width = rows.shape[1]
    top = rows[:TOP]
    lane_head = lax.broadcasted_iota(jnp.int32, (TOP, width), 1) >> DH_BITS
    pieces = [jnp.where(lane_head == h, top, 0.0) for h in range(H)]
    rest = rows[TOP:A]
    rest = jnp.concatenate([rest, rest], axis=0)
    lane_head = lax.broadcasted_iota(jnp.int32, (8, width), 1) >> DH_BITS
    upper = lax.broadcasted_iota(jnp.int32, (8, width), 0) >> 2
    pieces += [jnp.where(lane_head == 2 * i + upper, rest, 0.0) for i in range(H // 2)]
    return jnp.concatenate(pieces, axis=0)


def spread_into(spread_ref, head_ref):
    level = lax.axis_index("dp") // PAIR
    head = head_ref[:, pl.ds(level, 1), :].reshape(A, H * DH)
    high, low = split_high(spread_heads(head))
    spread_ref[:SPREAD, :] = high
    spread_ref[SPREAD:, :] = low
    return head


def fold_into(out_ref, proj_ref, spread_ref, parts):
    product = dot_nt(spread_ref[...], proj_ref[...])
    product = product[:SPREAD] + product[SPREAD:]
    if parts == 1:
        out_ref[...] = product.astype(BF16)
    else:
        high, low = split_high(product)
        out_ref[:SPREAD] = high
        out_ref[SPREAD:] = low


def spread_kernel(head_ref, spread_ref, head_buf, sem):
    copy = pltpu.make_async_copy(head_ref, head_buf, sem)
    copy.start()
    copy.wait()
    spread_into(spread_ref, head_buf)


def prior_kernel(spread_ref, proj_ref, out_ref):
    fold_into(out_ref, proj_ref, spread_ref, 1)


IN_HBM = pl.BlockSpec(memory_space=pltpu.HBM)
IN_VMEM = pl.BlockSpec(memory_space=pltpu.VMEM)


def head_spread(head_t):
    width = head_t.shape[2]
    return pl.pallas_call(
        spread_kernel,
        in_specs=[IN_HBM],
        out_specs=IN_VMEM,
        out_shape=jax.ShapeDtypeStruct((2 * SPREAD, width), BF16),
        scratch_shapes=[pltpu.VMEM(head_t.shape, F32), pltpu.SemaphoreType.DMA],
        compiler_params=pltpu.CompilerParams(vmem_limit_bytes=SPREAD_MIB * MIB),
        cost_estimate=pl.CostEstimate(
            flops=SPREAD_COST * SPREAD * width, bytes_accessed=4 * head_t.size, transcendentals=0
        ),
    )(head_t)


def prior_fold(spread, proj):
    depth, width = proj.shape
    return pl.pallas_call(
        prior_kernel,
        in_specs=[IN_VMEM, IN_VMEM],
        out_specs=IN_VMEM,
        out_shape=jax.ShapeDtypeStruct((SPREAD, depth), BF16),
        compiler_params=pltpu.CompilerParams(vmem_limit_bytes=PRIOR_MIB * MIB),
        cost_estimate=pl.CostEstimate(
            flops=PRIOR_COST * SPREAD * depth * width,
            bytes_accessed=2 * depth * width,
            transcendentals=0,
        ),
    )(spread, proj)


def pool_into(out_ref, tokens_ref, query_ref, prior_ref):
    count = tokens_ref.shape[0]
    half = out_ref.shape[3]
    block = BLOCK_ROWS * OBS
    blocks = count // block
    device_place = lax.axis_index("dp")
    level = device_place // PAIR
    lower = jnp.maximum(level - 1, 0)
    queries = jnp.concatenate(
        [query_ref[level].astype(F32), prior_ref[lower].astype(F32)], axis=0
    ).astype(BF16)
    row_of = lax.broadcasted_iota(jnp.int32, (block, block), 0) >> OBS_BITS
    column_of = lax.broadcasted_iota(jnp.int32, (block, block), 1) >> OBS_BITS
    same_row = (row_of == column_of).astype(F32).astype(BF16)
    mask = (
        lax.broadcasted_iota(jnp.int32, (BLOCK_ROWS, block), 0)
        == lax.broadcasted_iota(jnp.int32, (BLOCK_ROWS, block), 1) >> OBS_BITS
    )
    start = pl.multiple_of(device_place % PAIR * half, half)
    scores = dot_nt(queries, tokens_ref[...])
    scores = [scores[:, i * block : (i + 1) * block] for i in range(blocks)]
    exp_scores = jnp.exp(5.0 * jnp.tanh(jnp.concatenate(scores, axis=0) / 5.0))
    first, rest = split_high(exp_scores)
    second, third = split_high(exp_scores - first.astype(F32))
    parts = dot_nn(jnp.concatenate([first, second, third], axis=0), same_row)
    rows = 2 * H * blocks
    total = parts[:rows] + parts[rows : 2 * rows] + parts[2 * rows :]
    attention = (exp_scores / total).astype(BF16).astype(F32)
    for i in range(blocks):
        at = 2 * H * i
        spread = jnp.concatenate(
            [jnp.where(mask, attention[at + j : at + j + 1], 0.0) for j in range(2 * H)], axis=0
        ).astype(BF16)
        pooled = dot_nn(spread, tokens_ref[i * block : (i + 1) * block, pl.ds(start, half)])
        out_ref[:, :, i * BLOCK_ROWS : (i + 1) * BLOCK_ROWS, :] = pooled.astype(BF16).reshape(
            2, H, BLOCK_ROWS, half
        )


def own_kernel(
    tokens_ref, query_ref, prior_ref, head_ref, proj_ref, pool_ref, map_ref, wide_ref, spread_ref
):
    head = spread_into(spread_ref, head_ref)
    fold_into(map_ref, proj_ref, spread_ref, 2)
    head = jnp.concatenate([head, jnp.zeros((PAD - A, H * DH), F32)], axis=0)
    lane_head = lax.broadcasted_iota(jnp.int32, (PAD, H * DH), 1) >> DH_BITS
    wide = [jnp.where(lane_head == h, head, 0.0) for h in range(H)]
    wide_ref[...] = jnp.concatenate(wide, axis=0).astype(BF16)
    pool_into(pool_ref, tokens_ref, query_ref, prior_ref)


def own_side(tokens, query_weight, query_prior, head_t, proj):
    count, width = tokens.shape
    half = proj.shape[0]
    return pl.pallas_call(
        own_kernel,
        in_specs=[IN_VMEM] * 5,
        out_specs=[IN_VMEM] * 3,
        out_shape=[
            jax.ShapeDtypeStruct((2, H, count // OBS, half), BF16),
            jax.ShapeDtypeStruct((2 * SPREAD, half), BF16),
            jax.ShapeDtypeStruct((H * PAD, H * DH), BF16),
        ],
        scratch_shapes=[pltpu.VMEM((2 * SPREAD, H * DH), BF16)],
        compiler_params=pltpu.CompilerParams(vmem_limit_bytes=OWN_MIB * MIB),
        cost_estimate=pl.CostEstimate(
            flops=2 * count * width * 2 * H + 4 * count * H * BLOCK_ROWS * half,
            bytes_accessed=4 * count * width,
            transcendentals=4 * count * H,
        ),
    )(tokens, query_weight, query_prior, head_t, proj)


def peer_kernel(
    tokens_ref, query_ref, prior_ref, map_ref, own_ref, legal_ref, label_ref, pool_ref, told_ref
):
    pool_into(pool_ref, tokens_ref, query_ref, prior_ref)
    tables = [map_ref[:SPREAD], map_ref[SPREAD:]]
    rows = own_ref.shape[2]
    told_ref[:PAD] = raw_sums(tables, [own_ref, pool_ref], 0)
    told_ref[PAD:] = jnp.zeros((PAD, 2 * rows), F32)
    told_ref[PAD : PAD + A, :rows] = legal_ref[...].astype(F32)
    told_ref[PAD + A : PAD + A + 1, :rows] = label_ref[...].astype(F32)


def peer_side(tokens, query_weight, query_prior, own_map, own_pool, legal_t, label):
    count, width = tokens.shape
    half = own_map.shape[1]
    return pl.pallas_call(
        peer_kernel,
        in_specs=[IN_VMEM] * 7,
        out_specs=[IN_VMEM] * 2,
        out_shape=[
            jax.ShapeDtypeStruct((2, H, count // OBS, half), BF16),
            jax.ShapeDtypeStruct((2 * PAD, 2 * count // OBS), F32),
        ],
        compiler_params=pltpu.CompilerParams(vmem_limit_bytes=PEER_MIB * MIB),
        cost_estimate=pl.CostEstimate(
            flops=2 * count * width * 2 * H + 4 * count * H * BLOCK_ROWS * half,
            bytes_accessed=2 * count * width + 2 * count * half,
            transcendentals=4 * count * H,
        ),
    )(tokens, query_weight, query_prior, own_map, own_pool, legal_t, label)


def finish_raw(top, rest):
    rest = rest[:8] + rest[8:]
    rest = rest + jnp.concatenate([rest[4:], rest[:4]], axis=0)
    return jnp.concatenate([top, rest], axis=0)


def raw_sums(tables, pools, which):
    rows = len(pools) * pools[0].shape[2]
    top = jnp.zeros((TOP, rows), F32)
    rest = jnp.zeros((TOP, rows), F32)
    place = lax.broadcasted_iota(jnp.int32, (TOP, rows), 0) >> 2
    for h in range(H):
        left = []
        for table in tables:
            left += [table[h * TOP : (h + 1) * TOP], table[H * TOP + h // 4 * TOP :][:TOP]]
        pooled = jnp.concatenate([pool[which, h] for pool in pools], axis=0)
        result = dot_nt(jnp.concatenate(left, axis=0), pooled)
        for i in range(len(tables)):
            top = top + result[2 * i * TOP :][:TOP]
            rest = rest + jnp.where(place == h % 4, result[(2 * i + 1) * TOP :][:TOP], 0.0)
    return finish_raw(top, rest)


def lower_kernel(map_ref, own_ref, peer_ref, earlier_ref, out_ref):
    out_ref[...] = raw_sums([map_ref[...]], [own_ref, peer_ref], 1)


def lower_raw(lower_map, own_pool, peer_pool, earlier):
    _, _, rows, half = own_pool.shape
    return pl.pallas_call(
        lower_kernel,
        in_specs=[IN_VMEM] * 4,
        out_specs=IN_VMEM,
        out_shape=jax.ShapeDtypeStruct((PAD, 2 * rows), F32),
        compiler_params=pltpu.CompilerParams(vmem_limit_bytes=12 * MIB),
        cost_estimate=pl.CostEstimate(
            flops=8 * TOP * rows * H * half, bytes_accessed=4 * rows * H * half, transcendentals=0
        ),
    )(lower_map, own_pool, peer_pool, earlier)


def policy_rows(raw, legal):
    logits = 30.0 * jnp.tanh(raw / 30.0)
    exp_logits = jnp.exp(logits) * legal
    partition = jnp.sum(exp_logits, axis=0, keepdims=True)
    return logits, exp_logits / partition, logits - jnp.log(partition)


def swapped(theirs):
    rows = theirs.shape[1] // 2
    return jnp.concatenate([theirs[:, rows:], theirs[:, :rows]], axis=1)


def grad_into(out_ref, loss_ref, out_buf, sems, mine_ref, theirs_ref, wide_ref, own_ref, peer_ref, lower):
    rows = own_ref.shape[2]
    told = jnp.concatenate([mine_ref[PAD:, :rows], theirs_ref[PAD:, :rows]], axis=1)
    move = lax.broadcasted_iota(jnp.int32, told.shape, 0)
    legal = jnp.where(move < A, told, 0.0)
    onehot = (move.astype(F32) == told[A : A + 1]).astype(F32)
    logits, policy, log_policy = policy_rows(mine_ref[:PAD] + swapped(theirs_ref[:PAD]), legal)
    if lower is None:
        partner = legal / jnp.sum(legal, axis=0, keepdims=True)
    else:
        partner = policy_rows(lower, legal)[1]
    target = 0.5 * onehot + 0.5 * partner
    loss = -jnp.sum(target * log_policy, axis=0, keepdims=True)
    loss_ref[...] = loss[:, :rows]
    logit_grad = (policy - target) * (1.0 - (logits / 30.0) ** 2)
    high, low = split_high(logit_grad)
    left = jnp.concatenate([high.astype(F32), low.astype(F32)], axis=0).astype(BF16)
    chunk = out_buf.shape[0] // GRAD_CHUNKS
    copies = []
    for i in range(GRAD_CHUNKS):
        columns = slice(i * chunk, (i + 1) * chunk)
        narrow = []
        for h in range(H):
            pooled = jnp.concatenate([own_ref[0, h, :, columns], peer_ref[0, h, :, columns]], axis=0)
            product = dot_nn(left, pooled)
            narrow.append(product[:PAD] + product[PAD:])
        narrow = jnp.concatenate(narrow, axis=0).astype(BF16)
        out_buf[columns, :] = dot_tn(narrow, wide_ref[...])
        part = pl.ds(i * chunk, chunk)
        copies.append(pltpu.make_async_copy(out_buf.at[part], out_ref.at[part], sems.at[i]))
        copies[i].start()
    for copy in copies:
        copy.wait()


def lowest_grad_kernel(
    mine_ref, theirs_ref, wide_ref, own_ref, peer_ref, out_ref, loss_ref, out_buf, sems
):
    @pl.when(lax.axis_index("dp") // PAIR == 0)
    def _():
        grad_into(
            out_ref, loss_ref, out_buf, sems,
            mine_ref, theirs_ref, wide_ref, own_ref, peer_ref, None,
        )


def upper_grad_kernel(
    mine_ref, theirs_ref, wide_ref, own_ref, peer_ref,
    lower_ref, lower_theirs_ref, lowest_ref, lowest_loss_ref,
    out_ref, loss_ref, out_buf, sems,
):
    level = lax.axis_index("dp") // PAIR

    @pl.when(level == 0)
    def _():
        loss_ref[...] = lowest_loss_ref[...]

    @pl.when(level > 0)
    def _():
        grad_into(
            out_ref, loss_ref, out_buf, sems,
            mine_ref, theirs_ref, wide_ref, own_ref, peer_ref,
            lower_ref[...] + swapped(lower_theirs_ref[...]),
        )


def gradient(kernel, operands, into):
    _, _, rows, half = operands[3].shape
    width = H * DH
    count = len(operands)
    return pl.pallas_call(
        kernel,
        in_specs=[IN_VMEM] * count + ([IN_HBM, IN_VMEM] if into else []),
        out_specs=[IN_HBM, IN_VMEM],
        out_shape=[
            jax.ShapeDtypeStruct((half, width), F32),
            jax.ShapeDtypeStruct((1, rows), F32),
        ],
        input_output_aliases={count: 0} if into else {},
        scratch_shapes=[
            pltpu.VMEM((half, width), F32),
            pltpu.SemaphoreType.DMA((GRAD_CHUNKS,)),
        ],
        compiler_params=pltpu.CompilerParams(vmem_limit_bytes=16 * MIB),
        cost_estimate=pl.CostEstimate(
            flops=2 * H * PAD * half * width,
            bytes_accessed=4 * half * width + 4 * rows * H * half,
            transcendentals=0,
        ),
    )(*operands, *into)


def rotated(block, axis, distance):
    count = lax.axis_size(axis)
    return lax.ppermute(block, axis, [(i, (i + distance) % count) for i in range(count)])


def paired_device(
    tokens, legal_moves, action_label, value_weight, value_prior,
    query_weight, query_prior, policy_head, head_prior,
):
    peer_tokens = partner_2(tokens, "dp", 0)
    spread = head_spread(jnp.transpose(head_prior, (1, 0, 2)))
    prior_map = prior_fold(spread, value_prior)
    lower_map = rotated(prior_map, "dp", PAIR)
    own_pool, own_map, wide = own_side(
        tokens, query_weight, query_prior, jnp.transpose(policy_head, (1, 0, 2)), value_weight
    )
    peer_pool, mine = peer_side(
        peer_tokens, query_weight, query_prior, own_map, own_pool,
        legal_moves.T, action_label.reshape(1, -1),
    )
    theirs = partner_2(mine, "dp", 0)
    operands = [mine, theirs, wide, own_pool, peer_pool]
    lowest = gradient(lowest_grad_kernel, operands, [])
    lower = lower_raw(lower_map, own_pool, peer_pool, lowest[1])
    lower_theirs = partner_2(lower, "dp", 0)
    weight_grad, row_loss = gradient(upper_grad_kernel, operands + [lower, lower_theirs], lowest)
    return weight_grad, row_loss.reshape(-1)


def solution(mesh):
    paired = mesh.shape["dp"] == LEVELS * PAIR
    return jax.shard_map(
        paired_device if paired else general_device,
        mesh=mesh,
        in_specs=(
            P(("groups", "dp"), None),
            P(("groups", "dp"), None),
            P(("groups", "dp")),
            P("dp", None),
            P("dp", None),
            P(),
            P(),
            P(),
            P(),
        ),
        out_specs=(P(("groups", "dp"), None), P(("groups", "dp"))),
        check_vma=False,
    )
```

```python
import jax
import jax.numpy as jnp
from jax import lax
from jax.experimental import pallas as pl
from jax.experimental.pallas import tpu as pltpu
from jax.sharding import PartitionSpec as P

H = 8
DH = 128
A = 20
OBS = 16
LEVELS = 8
EXACT = lax.Precision.HIGHEST


def partner_2(block, axis, bit):
    count = lax.axis_size(axis)
    route = []
    for low in range(count):
        high = low | 1 << bit
        if high != low and high < count:
            route += [(low, high), (high, low)]
    return lax.ppermute(block, axis, route)


def shifted(block, axis, distance):
    devices = range(lax.axis_size(axis))
    route = [(i - distance, i) for i in devices if i - distance in devices]
    return lax.ppermute(block, axis, route)


def head_map(proj, move_head):
    depth = proj.shape[0]
    product = jnp.einsum(
        "dhe,ahe->had",
        proj.astype(jnp.float32).reshape(depth, H, DH),
        move_head.reshape(A, H, DH),
        precision=EXACT,
    )
    return product.reshape(H * A, depth).astype(jnp.bfloat16)


def gather_columns(block, member, bit_count):
    for bit_place in range(bit_count):
        received = partner_2(block, "dp", bit_place)
        upper_side = member // (1 << bit_place) % 2 == 1
        lower_half = jnp.where(upper_side, received, block)
        upper_half = jnp.where(upper_side, block, received)
        block = jnp.concatenate([lower_half, upper_half], axis=1)
    return block


def scatter_columns(block, member, bit_count):
    for bit_place in reversed(range(bit_count)):
        half = block.shape[1] // 2
        upper_side = member // (1 << bit_place) % 2 == 1
        kept = jnp.where(upper_side, block[:, half:], block[:, :half])
        sent = jnp.where(upper_side, block[:, :half], block[:, half:])
        block = kept + partner_2(sent, "dp", bit_place)
    return block


def attention_of(tokens, query_proj):
    scores = lax.dot_general(
        tokens, query_proj, (((1,), (1,)), ((), ())), preferred_element_type=jnp.float32
    ).reshape(-1, OBS, H)
    exp_scores = jnp.exp(5.0 * jnp.tanh(scores / 5.0))
    attention = exp_scores / jnp.sum(exp_scores, axis=1, keepdims=True)
    return attention.astype(jnp.bfloat16).astype(jnp.float32)


def policy_of(tokens, attention, mapped, legal_float):
    row_count = legal_float.shape[0]
    moved = lax.dot_general(
        tokens, mapped, (((1,), (1,)), ((), ())), preferred_element_type=jnp.float32
    ).reshape(row_count, OBS, H, A)
    raw_logits = jnp.sum(attention[..., None] * moved, axis=(1, 2))
    logits = 30.0 * jnp.tanh(raw_logits / 30.0)
    exp_logits = jnp.exp(logits) * legal_float
    partition = jnp.sum(exp_logits, axis=1, keepdims=True)
    return logits, exp_logits / partition, logits - jnp.log(partition)


def general_device(
    tokens, legal_moves, action_label, value_weight, value_prior,
    query_weight, query_prior, policy_head, head_prior,
):
    group_size = lax.axis_size("dp") // LEVELS
    bit_count = group_size.bit_length() - 1
    device_place = lax.axis_index("dp")
    level_index = device_place // group_size
    member = device_place % group_size
    lower_index = jnp.maximum(level_index - 1, 0)

    def of_level(array, index):
        return lax.dynamic_index_in_dim(array, index, 0, keepdims=False)

    move_head = of_level(policy_head, level_index)
    prior_map = head_map(value_prior, of_level(head_prior, level_index))
    own_map = head_map(value_weight, move_head)
    lower_map = gather_columns(shifted(prior_map, "dp", group_size), member, bit_count)
    own_map = gather_columns(own_map, member, bit_count)
    attention = attention_of(tokens, of_level(query_weight, level_index))
    lower_attention = attention_of(tokens, of_level(query_prior, lower_index))
    legal_float = legal_moves.astype(jnp.float32)
    logits, policy, log_policy = policy_of(tokens, attention, own_map, legal_float)
    _, lower_policy, _ = policy_of(tokens, lower_attention, lower_map, legal_float)
    uniform_policy = legal_float / jnp.sum(legal_float, axis=1, keepdims=True)
    partner = jnp.where(level_index == 0, uniform_policy, lower_policy)
    onehot = (action_label[:, None] == jnp.arange(A, dtype=jnp.int32)[None, :]).astype(jnp.float32)
    target = 0.5 * onehot + 0.5 * partner
    row_loss = -jnp.sum(target * log_policy, axis=1)
    logit_grad = (policy - target) * (1.0 - (logits / 30.0) ** 2)
    token_grad = attention[..., None] * logit_grad[:, None, None, :]
    token_grad = token_grad.astype(jnp.bfloat16).reshape(tokens.shape[0], H * A)
    mapped_grad = lax.dot_general(
        token_grad, tokens, (((0,), (0,)), ((), ())), preferred_element_type=jnp.float32
    )
    mapped_grad = scatter_columns(mapped_grad, member, bit_count).reshape(H, A, -1)
    weight_grad = jnp.einsum(
        "had,ahe->dhe", mapped_grad, move_head.reshape(A, H, DH), precision=EXACT
    )
    return weight_grad.reshape(-1, H * DH), row_loss


PAIR = 2
TOP = 16
SPREAD = H * A
BLOCK_ROWS = 16
F32 = jnp.float32
BF16 = jnp.bfloat16
PAD = 24
GRAD_CHUNKS = 4
DH_BITS = 7
OBS_BITS = 4
MIB = 2**20
PRIOR_MIB = 12
OWN_MIB = 16
PEER_MIB = 16
PRIOR_COST = 40
SPREAD_COST = 100000
SPREAD_MIB = 53


def dot_nt(left, right):
    return lax.dot_general(left, right, (((1,), (1,)), ((), ())), preferred_element_type=F32)


def dot_nn(left, right):
    return lax.dot_general(left, right, (((1,), (0,)), ((), ())), preferred_element_type=F32)


def dot_tn(left, right):
    return lax.dot_general(
        left, right, (((0,), (0,)), ((), ())), preferred_element_type=F32
    )


def split_high(value):
    high = value.astype(BF16)
    return high, (value - high.astype(F32)).astype(BF16)


def spread_heads(rows):
    width = rows.shape[1]
    top = rows[:TOP]
    lane_head = lax.broadcasted_iota(jnp.int32, (TOP, width), 1) >> DH_BITS
    pieces = [jnp.where(lane_head == h, top, 0.0) for h in range(H)]
    rest = rows[TOP:A]
    rest = jnp.concatenate([rest, rest], axis=0)
    lane_head = lax.broadcasted_iota(jnp.int32, (8, width), 1) >> DH_BITS
    upper = lax.broadcasted_iota(jnp.int32, (8, width), 0) >> 2
    pieces += [jnp.where(lane_head == 2 * i + upper, rest, 0.0) for i in range(H // 2)]
    return jnp.concatenate(pieces, axis=0)


def level_head(head_ref):
    level = lax.axis_index("dp") // PAIR
    return head_ref[:, pl.ds(level, 1), :].reshape(A, H * DH)


def spread_into(spread_ref, head):
    high, low = split_high(spread_heads(head))
    spread_ref[:SPREAD, :] = high
    spread_ref[SPREAD:, :] = low


def fold_into(out_ref, proj_ref, spread_ref, parts):
    product = dot_nt(spread_ref[...], proj_ref[...])
    product = product[:SPREAD] + product[SPREAD:]
    if parts == 1:
        out_ref[...] = product.astype(BF16)
    else:
        high, low = split_high(product)
        out_ref[:SPREAD] = high
        out_ref[SPREAD:] = low


def spread_kernel(head_ref, spread_ref, head_buf, sem):
    level = lax.axis_index("dp") // PAIR
    copy = pltpu.make_async_copy(head_ref.at[:, pl.ds(level, 1)], head_buf, sem)
    copy.start()
    copy.wait()
    spread_into(spread_ref, head_buf[...].reshape(A, H * DH))


def prior_kernel(spread_ref, proj_ref, out_ref):
    fold_into(out_ref, proj_ref, spread_ref, 1)


IN_HBM = pl.BlockSpec(memory_space=pltpu.HBM)
IN_VMEM = pl.BlockSpec(memory_space=pltpu.VMEM)


def head_spread(head_t):
    width = head_t.shape[2]
    return pl.pallas_call(
        spread_kernel,
        in_specs=[IN_HBM],
        out_specs=IN_VMEM,
        out_shape=jax.ShapeDtypeStruct((2 * SPREAD, width), BF16),
        scratch_shapes=[pltpu.VMEM((A, 1, width), F32), pltpu.SemaphoreType.DMA],
        compiler_params=pltpu.CompilerParams(vmem_limit_bytes=SPREAD_MIB * MIB),
        cost_estimate=pl.CostEstimate(
            flops=SPREAD_COST * SPREAD * width, bytes_accessed=4 * head_t.size, transcendentals=0
        ),
    )(head_t)


def prior_fold(spread, proj):
    depth, width = proj.shape
    return pl.pallas_call(
        prior_kernel,
        in_specs=[IN_VMEM, IN_VMEM],
        out_specs=IN_VMEM,
        out_shape=jax.ShapeDtypeStruct((SPREAD, depth), BF16),
        compiler_params=pltpu.CompilerParams(vmem_limit_bytes=PRIOR_MIB * MIB),
        cost_estimate=pl.CostEstimate(
            flops=PRIOR_COST * SPREAD * depth * width,
            bytes_accessed=2 * depth * width,
            transcendentals=0,
        ),
    )(spread, proj)


def pool_into(out_ref, tokens_ref, query_ref, prior_ref):
    count = tokens_ref.shape[0]
    half = out_ref.shape[3]
    block = BLOCK_ROWS * OBS
    blocks = count // block
    device_place = lax.axis_index("dp")
    level = device_place // PAIR
    lower = jnp.maximum(level - 1, 0)
    queries = jnp.concatenate(
        [query_ref[level].astype(F32), prior_ref[lower].astype(F32)], axis=0
    ).astype(BF16)
    row_of = lax.broadcasted_iota(jnp.int32, (block, block), 0) >> OBS_BITS
    column_of = lax.broadcasted_iota(jnp.int32, (block, block), 1) >> OBS_BITS
    same_row = (row_of == column_of).astype(F32).astype(BF16)
    mask = (
        lax.broadcasted_iota(jnp.int32, (BLOCK_ROWS, block), 0)
        == lax.broadcasted_iota(jnp.int32, (BLOCK_ROWS, block), 1) >> OBS_BITS
    )
    start = pl.multiple_of(device_place % PAIR * half, half)
    scores = dot_nt(queries, tokens_ref[...])
    scores = [scores[:, i * block : (i + 1) * block] for i in range(blocks)]
    exp_scores = jnp.exp(5.0 * jnp.tanh(jnp.concatenate(scores, axis=0) / 5.0))
    first, rest = split_high(exp_scores)
    second, third = split_high(exp_scores - first.astype(F32))
    parts = dot_nn(jnp.concatenate([first, second, third], axis=0), same_row)
    rows = 2 * H * blocks
    total = parts[:rows] + parts[rows : 2 * rows] + parts[2 * rows :]
    attention = (exp_scores / total).astype(BF16).astype(F32)
    for i in range(blocks):
        at = 2 * H * i
        spread = jnp.concatenate(
            [jnp.where(mask, attention[at + j : at + j + 1], 0.0) for j in range(2 * H)], axis=0
        ).astype(BF16)
        pooled = dot_nn(spread, tokens_ref[i * block : (i + 1) * block, pl.ds(start, half)])
        out_ref[:, :, i * BLOCK_ROWS : (i + 1) * BLOCK_ROWS, :] = pooled.astype(BF16).reshape(
            2, H, BLOCK_ROWS, half
        )


def own_kernel(
    tokens_ref, query_ref, prior_ref, head_ref, proj_ref, pool_ref, map_ref, wide_ref, spread_ref
):
    head = level_head(head_ref)
    spread_into(spread_ref, head)
    fold_into(map_ref, proj_ref, spread_ref, 2)
    head = jnp.concatenate([head, jnp.zeros((PAD - A, H * DH), F32)], axis=0)
    lane_head = lax.broadcasted_iota(jnp.int32, (PAD, H * DH), 1) >> DH_BITS
    wide = [jnp.where(lane_head == h, head, 0.0) for h in range(H)]
    wide_ref[...] = jnp.concatenate(wide, axis=0).astype(BF16)
    pool_into(pool_ref, tokens_ref, query_ref, prior_ref)


def own_side(tokens, query_weight, query_prior, head_t, proj):
    count, width = tokens.shape
    half = proj.shape[0]
    return pl.pallas_call(
        own_kernel,
        in_specs=[IN_VMEM] * 5,
        out_specs=[IN_VMEM] * 3,
        out_shape=[
            jax.ShapeDtypeStruct((2, H, count // OBS, half), BF16),
            jax.ShapeDtypeStruct((2 * SPREAD, half), BF16),
            jax.ShapeDtypeStruct((H * PAD, H * DH), BF16),
        ],
        scratch_shapes=[pltpu.VMEM((2 * SPREAD, H * DH), BF16)],
        compiler_params=pltpu.CompilerParams(vmem_limit_bytes=OWN_MIB * MIB),
        cost_estimate=pl.CostEstimate(
            flops=2 * count * width * 2 * H + 4 * count * H * BLOCK_ROWS * half,
            bytes_accessed=4 * count * width,
            transcendentals=4 * count * H,
        ),
    )(tokens, query_weight, query_prior, head_t, proj)


def peer_kernel(
    tokens_ref, query_ref, prior_ref, map_ref, own_ref, legal_ref, label_ref, pool_ref, told_ref
):
    pool_into(pool_ref, tokens_ref, query_ref, prior_ref)
    tables = [map_ref[:SPREAD], map_ref[SPREAD:]]
    rows = own_ref.shape[2]
    told_ref[:PAD] = raw_sums(tables, [own_ref, pool_ref], 0)
    told_ref[PAD:] = jnp.zeros((PAD, 2 * rows), F32)
    told_ref[PAD : PAD + A, :rows] = legal_ref[...].astype(F32)
    told_ref[PAD + A : PAD + A + 1, :rows] = label_ref[...].astype(F32)


def peer_side(tokens, query_weight, query_prior, own_map, own_pool, legal_t, label):
    count, width = tokens.shape
    half = own_map.shape[1]
    return pl.pallas_call(
        peer_kernel,
        in_specs=[IN_VMEM] * 7,
        out_specs=[IN_VMEM] * 2,
        out_shape=[
            jax.ShapeDtypeStruct((2, H, count // OBS, half), BF16),
            jax.ShapeDtypeStruct((2 * PAD, 2 * count // OBS), F32),
        ],
        compiler_params=pltpu.CompilerParams(vmem_limit_bytes=PEER_MIB * MIB),
        cost_estimate=pl.CostEstimate(
            flops=2 * count * width * 2 * H + 4 * count * H * BLOCK_ROWS * half,
            bytes_accessed=2 * count * width + 2 * count * half,
            transcendentals=4 * count * H,
        ),
    )(tokens, query_weight, query_prior, own_map, own_pool, legal_t, label)


def finish_raw(top, rest):
    rest = rest[:8] + rest[8:]
    rest = rest + jnp.concatenate([rest[4:], rest[:4]], axis=0)
    return jnp.concatenate([top, rest], axis=0)


def raw_sums(tables, pools, which):
    rows = len(pools) * pools[0].shape[2]
    top = jnp.zeros((TOP, rows), F32)
    rest = jnp.zeros((TOP, rows), F32)
    place = lax.broadcasted_iota(jnp.int32, (TOP, rows), 0) >> 2
    for h in range(H):
        left = []
        for table in tables:
            left += [table[h * TOP : (h + 1) * TOP], table[H * TOP + h // 4 * TOP :][:TOP]]
        pooled = jnp.concatenate([pool[which, h] for pool in pools], axis=0)
        result = dot_nt(jnp.concatenate(left, axis=0), pooled)
        for i in range(len(tables)):
            top = top + result[2 * i * TOP :][:TOP]
            rest = rest + jnp.where(place == h % 4, result[(2 * i + 1) * TOP :][:TOP], 0.0)
    return finish_raw(top, rest)


def lower_kernel(map_ref, own_ref, peer_ref, earlier_ref, out_ref):
    level = lax.axis_index("dp") // PAIR

    @pl.when(level == 0)
    def _():
        out_ref[...] = jnp.zeros_like(out_ref)

    @pl.when(level > 0)
    def _():
        out_ref[...] = raw_sums([map_ref[...]], [own_ref, peer_ref], 1)


def lower_raw(lower_map, own_pool, peer_pool, earlier):
    _, _, rows, half = own_pool.shape
    return pl.pallas_call(
        lower_kernel,
        in_specs=[IN_VMEM] * 4,
        out_specs=IN_VMEM,
        out_shape=jax.ShapeDtypeStruct((PAD, 2 * rows), F32),
        compiler_params=pltpu.CompilerParams(vmem_limit_bytes=12 * MIB),
        cost_estimate=pl.CostEstimate(
            flops=8 * TOP * rows * H * half, bytes_accessed=4 * rows * H * half, transcendentals=0
        ),
    )(lower_map, own_pool, peer_pool, earlier)


def policy_rows(raws, legal):
    squashed = jnp.tanh(jnp.concatenate(raws, axis=0) * (1.0 / 30.0))
    logits = 30.0 * squashed
    exp_logits = jnp.exp(logits)
    found = []
    for i in range(len(raws)):
        rows = slice(i * PAD, (i + 1) * PAD)
        weights = exp_logits[rows] * legal
        partition = jnp.sum(weights, axis=0, keepdims=True)
        found.append((squashed[rows], logits[rows], weights * (1.0 / partition), partition))
    return found


def swapped(theirs):
    rows = theirs.shape[1] // 2
    return jnp.concatenate([theirs[:, rows:], theirs[:, :rows]], axis=1)


def grad_into(out_ref, loss_ref, out_buf, loss_buf, sems, mine_ref, theirs_ref, wide_ref, own_ref, peer_ref, lower):
    rows = own_ref.shape[2]
    told = jnp.concatenate([mine_ref[PAD:, :rows], theirs_ref[PAD:, :rows]], axis=1)
    move = lax.broadcasted_iota(jnp.int32, told.shape, 0)
    legal = jnp.where(move < A, told, 0.0)
    onehot = (move.astype(F32) == told[A : A + 1]).astype(F32)
    raws = [mine_ref[:PAD] + swapped(theirs_ref[:PAD])] + lower
    found = policy_rows(raws, legal)
    squashed, logits, policy, partition = found[0]
    if lower:
        partner = found[1][2]
    else:
        partner = legal * (1.0 / jnp.sum(legal, axis=0, keepdims=True))
    target = 0.5 * onehot + 0.5 * partner
    log_policy = logits - jnp.log(partition)
    loss = -jnp.sum(target * log_policy, axis=0, keepdims=True)
    loss_buf[...] = loss[:, :rows]
    loss_copy = pltpu.make_async_copy(loss_buf, loss_ref, sems.at[GRAD_CHUNKS])
    loss_copy.start()
    logit_grad = (policy - target) * (1.0 - squashed * squashed)
    high, low = split_high(logit_grad)
    left = jnp.concatenate([high.astype(F32), low.astype(F32)], axis=0).astype(BF16)
    chunk = out_buf.shape[0] // GRAD_CHUNKS
    copies = []
    for i in range(GRAD_CHUNKS):
        columns = slice(i * chunk, (i + 1) * chunk)
        narrow = []
        for h in range(H):
            pooled = jnp.concatenate([own_ref[0, h, :, columns], peer_ref[0, h, :, columns]], axis=0)
            product = dot_nn(left, pooled)
            narrow.append(product[:PAD] + product[PAD:])
        narrow = jnp.concatenate(narrow, axis=0).astype(BF16)
        out_buf[columns, :] = dot_tn(narrow, wide_ref[...])
        part = pl.ds(i * chunk, chunk)
        copies.append(pltpu.make_async_copy(out_buf.at[part], out_ref.at[part], sems.at[i]))
        copies[i].start()
    for copy in copies + [loss_copy]:
        copy.wait()


def lowest_grad_kernel(
    mine_ref, theirs_ref, wide_ref, own_ref, peer_ref,
    out_ref, loss_ref, token_ref, out_buf, loss_buf, sems,
):
    token_ref[...] = jnp.zeros_like(token_ref)

    @pl.when(lax.axis_index("dp") // PAIR == 0)
    def _():
        grad_into(
            out_ref, loss_ref, out_buf, loss_buf, sems,
            mine_ref, theirs_ref, wide_ref, own_ref, peer_ref, [],
        )


def upper_grad_kernel(
    mine_ref, theirs_ref, wide_ref, own_ref, peer_ref,
    lower_ref, lower_theirs_ref, lowest_ref, lowest_loss_ref,
    out_ref, loss_ref, out_buf, loss_buf, sems,
):
    @pl.when(lax.axis_index("dp") // PAIR > 0)
    def _():
        grad_into(
            out_ref, loss_ref, out_buf, loss_buf, sems,
            mine_ref, theirs_ref, wide_ref, own_ref, peer_ref,
            [lower_ref[...] + swapped(lower_theirs_ref[...])],
        )


def gradient(kernel, operands, into):
    _, _, rows, half = operands[3].shape
    width = H * DH
    count = len(operands)
    return pl.pallas_call(
        kernel,
        in_specs=[IN_VMEM] * count + [IN_HBM] * len(into),
        out_specs=[IN_HBM, IN_HBM] + ([] if into else [IN_VMEM]),
        out_shape=[
            jax.ShapeDtypeStruct((half, width), F32),
            jax.ShapeDtypeStruct((1, rows), F32),
        ]
        + ([] if into else [jax.ShapeDtypeStruct((8, DH), F32)]),
        input_output_aliases={count + i: i for i in range(len(into))},
        scratch_shapes=[
            pltpu.VMEM((half, width), F32),
            pltpu.VMEM((1, rows), F32),
            pltpu.SemaphoreType.DMA((GRAD_CHUNKS + 1,)),
        ],
        compiler_params=pltpu.CompilerParams(vmem_limit_bytes=16 * MIB),
        cost_estimate=pl.CostEstimate(
            flops=2 * H * PAD * half * width,
            bytes_accessed=4 * half * width + 4 * rows * H * half,
            transcendentals=0,
        ),
    )(*operands, *into)


def rotated(block, axis, distance):
    count = lax.axis_size(axis)
    return lax.ppermute(block, axis, [(i, (i + distance) % count) for i in range(count)])


def paired_device(
    tokens, legal_moves, action_label, value_weight, value_prior,
    query_weight, query_prior, policy_head, head_prior,
):
    peer_tokens = partner_2(tokens, "dp", 0)
    spread = head_spread(jnp.transpose(head_prior, (1, 0, 2)))
    prior_map = prior_fold(spread, value_prior)
    lower_map = rotated(prior_map, "dp", PAIR)
    own_pool, own_map, wide = own_side(
        tokens, query_weight, query_prior, jnp.transpose(policy_head, (1, 0, 2)), value_weight
    )
    peer_pool, mine = peer_side(
        peer_tokens, query_weight, query_prior, own_map, own_pool,
        legal_moves.T, action_label.reshape(1, -1),
    )
    theirs = partner_2(mine, "dp", 0)
    operands = [mine, theirs, wide, own_pool, peer_pool]
    *lowest, token = gradient(lowest_grad_kernel, operands, [])
    lower = lower_raw(lower_map, own_pool, peer_pool, token)
    lower_theirs = partner_2(lower, "dp", 0)
    weight_grad, row_loss = gradient(upper_grad_kernel, operands + [lower, lower_theirs], lowest)
    return weight_grad, row_loss.reshape(-1)


def solution(mesh):
    paired = mesh.shape["dp"] == LEVELS * PAIR
    return jax.shard_map(
        paired_device if paired else general_device,
        mesh=mesh,
        in_specs=(
            P(("groups", "dp"), None),
            P(("groups", "dp"), None),
            P(("groups", "dp")),
            P("dp", None),
            P("dp", None),
            P(),
            P(),
            P(),
            P(),
        ),
        out_specs=(P(("groups", "dp"), None), P(("groups", "dp"))),
        check_vma=False,
    )
```

```python
import jax
import jax.numpy as jnp
from jax import lax
from jax.experimental import pallas as pl
from jax.experimental.pallas import tpu as pltpu
from jax.sharding import PartitionSpec as P

H = 8
DH = 128
A = 20
OBS = 16
LEVELS = 8
EXACT = lax.Precision.HIGHEST


def partner_2(block, axis, bit):
    count = lax.axis_size(axis)
    route = []
    for low in range(count):
        high = low | 1 << bit
        if high != low and high < count:
            route += [(low, high), (high, low)]
    return lax.ppermute(block, axis, route)


def shifted(block, axis, distance):
    devices = range(lax.axis_size(axis))
    route = [(i - distance, i) for i in devices if i - distance in devices]
    return lax.ppermute(block, axis, route)


def head_map(proj, move_head):
    depth = proj.shape[0]
    product = jnp.einsum(
        "dhe,ahe->had",
        proj.astype(jnp.float32).reshape(depth, H, DH),
        move_head.reshape(A, H, DH),
        precision=EXACT,
    )
    return product.reshape(H * A, depth).astype(jnp.bfloat16)


def gather_columns(block, member, bit_count):
    for bit_place in range(bit_count):
        received = partner_2(block, "dp", bit_place)
        upper_side = member // (1 << bit_place) % 2 == 1
        lower_half = jnp.where(upper_side, received, block)
        upper_half = jnp.where(upper_side, block, received)
        block = jnp.concatenate([lower_half, upper_half], axis=1)
    return block


def scatter_columns(block, member, bit_count):
    for bit_place in reversed(range(bit_count)):
        half = block.shape[1] // 2
        upper_side = member // (1 << bit_place) % 2 == 1
        kept = jnp.where(upper_side, block[:, half:], block[:, :half])
        sent = jnp.where(upper_side, block[:, :half], block[:, half:])
        block = kept + partner_2(sent, "dp", bit_place)
    return block


def attention_of(tokens, query_proj):
    scores = lax.dot_general(
        tokens, query_proj, (((1,), (1,)), ((), ())), preferred_element_type=jnp.float32
    ).reshape(-1, OBS, H)
    exp_scores = jnp.exp(5.0 * jnp.tanh(scores / 5.0))
    attention = exp_scores / jnp.sum(exp_scores, axis=1, keepdims=True)
    return attention.astype(jnp.bfloat16).astype(jnp.float32)


def policy_of(tokens, attention, mapped, legal_float):
    row_count = legal_float.shape[0]
    moved = lax.dot_general(
        tokens, mapped, (((1,), (1,)), ((), ())), preferred_element_type=jnp.float32
    ).reshape(row_count, OBS, H, A)
    raw_logits = jnp.sum(attention[..., None] * moved, axis=(1, 2))
    logits = 30.0 * jnp.tanh(raw_logits / 30.0)
    exp_logits = jnp.exp(logits) * legal_float
    partition = jnp.sum(exp_logits, axis=1, keepdims=True)
    return logits, exp_logits / partition, logits - jnp.log(partition)


def general_device(
    tokens, legal_moves, action_label, value_weight, value_prior,
    query_weight, query_prior, policy_head, head_prior,
):
    group_size = lax.axis_size("dp") // LEVELS
    bit_count = group_size.bit_length() - 1
    device_place = lax.axis_index("dp")
    level_index = device_place // group_size
    member = device_place % group_size
    lower_index = jnp.maximum(level_index - 1, 0)

    def of_level(array, index):
        return lax.dynamic_index_in_dim(array, index, 0, keepdims=False)

    move_head = of_level(policy_head, level_index)
    prior_map = head_map(value_prior, of_level(head_prior, level_index))
    own_map = head_map(value_weight, move_head)
    lower_map = gather_columns(shifted(prior_map, "dp", group_size), member, bit_count)
    own_map = gather_columns(own_map, member, bit_count)
    attention = attention_of(tokens, of_level(query_weight, level_index))
    lower_attention = attention_of(tokens, of_level(query_prior, lower_index))
    legal_float = legal_moves.astype(jnp.float32)
    logits, policy, log_policy = policy_of(tokens, attention, own_map, legal_float)
    _, lower_policy, _ = policy_of(tokens, lower_attention, lower_map, legal_float)
    uniform_policy = legal_float / jnp.sum(legal_float, axis=1, keepdims=True)
    partner = jnp.where(level_index == 0, uniform_policy, lower_policy)
    onehot = (action_label[:, None] == jnp.arange(A, dtype=jnp.int32)[None, :]).astype(jnp.float32)
    target = 0.5 * onehot + 0.5 * partner
    row_loss = -jnp.sum(target * log_policy, axis=1)
    logit_grad = (policy - target) * (1.0 - (logits / 30.0) ** 2)
    token_grad = attention[..., None] * logit_grad[:, None, None, :]
    token_grad = token_grad.astype(jnp.bfloat16).reshape(tokens.shape[0], H * A)
    mapped_grad = lax.dot_general(
        token_grad, tokens, (((0,), (0,)), ((), ())), preferred_element_type=jnp.float32
    )
    mapped_grad = scatter_columns(mapped_grad, member, bit_count).reshape(H, A, -1)
    weight_grad = jnp.einsum(
        "had,ahe->dhe", mapped_grad, move_head.reshape(A, H, DH), precision=EXACT
    )
    return weight_grad.reshape(-1, H * DH), row_loss


PAIR = 2
TOP = 16
SPREAD = H * A
BLOCK_ROWS = 16
F32 = jnp.float32
BF16 = jnp.bfloat16
PAD = 24
GRAD_CHUNKS = 4
DH_BITS = 7
OBS_BITS = 4
MIB = 2**20
PRIOR_MIB = 12
OWN_MIB = 16
PEER_MIB = 16
PRIOR_COST = 40
SPREAD_COST = 100000
SPREAD_MIB = 53


def dot_nt(left, right):
    return lax.dot_general(left, right, (((1,), (1,)), ((), ())), preferred_element_type=F32)


def dot_nn(left, right):
    return lax.dot_general(left, right, (((1,), (0,)), ((), ())), preferred_element_type=F32)


def dot_tn(left, right):
    return lax.dot_general(
        left, right, (((0,), (0,)), ((), ())), preferred_element_type=F32
    )


def split_high(value):
    high = value.astype(BF16)
    return high, (value - high.astype(F32)).astype(BF16)


def spread_heads(rows):
    width = rows.shape[1]
    top = rows[:TOP]
    lane_head = lax.broadcasted_iota(jnp.int32, (TOP, width), 1) >> DH_BITS
    pieces = [jnp.where(lane_head == h, top, 0.0) for h in range(H)]
    rest = rows[TOP:A]
    rest = jnp.concatenate([rest, rest], axis=0)
    lane_head = lax.broadcasted_iota(jnp.int32, (8, width), 1) >> DH_BITS
    upper = lax.broadcasted_iota(jnp.int32, (8, width), 0) >> 2
    pieces += [jnp.where(lane_head == 2 * i + upper, rest, 0.0) for i in range(H // 2)]
    return jnp.concatenate(pieces, axis=0)


def level_head(head_ref):
    level = lax.axis_index("dp") // PAIR
    return head_ref[:, pl.ds(level, 1), :].reshape(A, H * DH)


def spread_into(spread_ref, head):
    high, low = split_high(spread_heads(head))
    spread_ref[:SPREAD, :] = high
    spread_ref[SPREAD:, :] = low


def fold_into(out_ref, proj_ref, spread_ref, parts):
    product = dot_nt(spread_ref[...], proj_ref[...])
    product = product[:SPREAD] + product[SPREAD:]
    if parts == 1:
        out_ref[...] = product.astype(BF16)
    else:
        high, low = split_high(product)
        out_ref[:SPREAD] = high
        out_ref[SPREAD:] = low


def spread_kernel(head_ref, spread_ref, head_buf, sem):
    level = lax.axis_index("dp") // PAIR
    copy = pltpu.make_async_copy(head_ref.at[:, pl.ds(level, 1)], head_buf, sem)
    copy.start()
    copy.wait()
    spread_into(spread_ref, head_buf[...].reshape(A, H * DH))


def prior_kernel(spread_ref, proj_ref, out_ref):
    fold_into(out_ref, proj_ref, spread_ref, 1)


IN_HBM = pl.BlockSpec(memory_space=pltpu.HBM)
IN_VMEM = pl.BlockSpec(memory_space=pltpu.VMEM)


def head_spread(head_t):
    width = head_t.shape[2]
    return pl.pallas_call(
        spread_kernel,
        in_specs=[IN_HBM],
        out_specs=IN_VMEM,
        out_shape=jax.ShapeDtypeStruct((2 * SPREAD, width), BF16),
        scratch_shapes=[pltpu.VMEM((A, 1, width), F32), pltpu.SemaphoreType.DMA],
        compiler_params=pltpu.CompilerParams(vmem_limit_bytes=SPREAD_MIB * MIB),
        cost_estimate=pl.CostEstimate(
            flops=SPREAD_COST * SPREAD * width, bytes_accessed=4 * head_t.size, transcendentals=0
        ),
    )(head_t)


def prior_fold(spread, proj):
    depth, width = proj.shape
    return pl.pallas_call(
        prior_kernel,
        in_specs=[IN_VMEM, IN_VMEM],
        out_specs=IN_VMEM,
        out_shape=jax.ShapeDtypeStruct((SPREAD, depth), BF16),
        compiler_params=pltpu.CompilerParams(vmem_limit_bytes=PRIOR_MIB * MIB),
        cost_estimate=pl.CostEstimate(
            flops=PRIOR_COST * SPREAD * depth * width,
            bytes_accessed=2 * depth * width,
            transcendentals=0,
        ),
    )(spread, proj)


def pool_into(out_ref, tokens_ref, query_ref, prior_ref):
    count = tokens_ref.shape[0]
    half = out_ref.shape[3]
    block = BLOCK_ROWS * OBS
    blocks = count // block
    device_place = lax.axis_index("dp")
    level = device_place // PAIR
    lower = jnp.maximum(level - 1, 0)
    queries = jnp.concatenate(
        [query_ref[level].astype(F32), prior_ref[lower].astype(F32)], axis=0
    ).astype(BF16)
    row_of = lax.broadcasted_iota(jnp.int32, (block, block), 0) >> OBS_BITS
    column_of = lax.broadcasted_iota(jnp.int32, (block, block), 1) >> OBS_BITS
    same_row = (row_of == column_of).astype(F32).astype(BF16)
    mask = (
        lax.broadcasted_iota(jnp.int32, (BLOCK_ROWS, block), 0)
        == lax.broadcasted_iota(jnp.int32, (BLOCK_ROWS, block), 1) >> OBS_BITS
    )
    start = pl.multiple_of(device_place % PAIR * half, half)
    scores = dot_nt(queries, tokens_ref[...])
    scores = [scores[:, i * block : (i + 1) * block] for i in range(blocks)]
    exp_scores = jnp.exp(5.0 * jnp.tanh(jnp.concatenate(scores, axis=0) / 5.0))
    first, rest = split_high(exp_scores)
    second, third = split_high(exp_scores - first.astype(F32))
    parts = dot_nn(jnp.concatenate([first, second, third], axis=0), same_row)
    rows = 2 * H * blocks
    total = parts[:rows] + parts[rows : 2 * rows] + parts[2 * rows :]
    attention = (exp_scores / total).astype(BF16).astype(F32)
    for i in range(blocks):
        at = 2 * H * i
        spread = jnp.concatenate(
            [jnp.where(mask, attention[at + j : at + j + 1], 0.0) for j in range(2 * H)], axis=0
        ).astype(BF16)
        pooled = dot_nn(spread, tokens_ref[i * block : (i + 1) * block, pl.ds(start, half)])
        out_ref[:, :, i * BLOCK_ROWS : (i + 1) * BLOCK_ROWS, :] = pooled.astype(BF16).reshape(
            2, H, BLOCK_ROWS, half
        )


def own_kernel(
    tokens_ref, query_ref, prior_ref, head_ref, proj_ref, pool_ref, map_ref, wide_ref, spread_ref
):
    head = level_head(head_ref)
    spread_into(spread_ref, head)
    fold_into(map_ref, proj_ref, spread_ref, 2)
    head = jnp.concatenate([head, jnp.zeros((PAD - A, H * DH), F32)], axis=0)
    lane_head = lax.broadcasted_iota(jnp.int32, (PAD, H * DH), 1) >> DH_BITS
    wide = [jnp.where(lane_head == h, head, 0.0) for h in range(H)]
    wide_ref[...] = jnp.concatenate(wide, axis=0).astype(BF16)
    pool_into(pool_ref, tokens_ref, query_ref, prior_ref)


def own_side(tokens, query_weight, query_prior, head_t, proj):
    count, width = tokens.shape
    half = proj.shape[0]
    return pl.pallas_call(
        own_kernel,
        in_specs=[IN_VMEM] * 5,
        out_specs=[IN_VMEM] * 3,
        out_shape=[
            jax.ShapeDtypeStruct((2, H, count // OBS, half), BF16),
            jax.ShapeDtypeStruct((2 * SPREAD, half), BF16),
            jax.ShapeDtypeStruct((H * PAD, H * DH), BF16),
        ],
        scratch_shapes=[pltpu.VMEM((2 * SPREAD, H * DH), BF16)],
        compiler_params=pltpu.CompilerParams(vmem_limit_bytes=OWN_MIB * MIB),
        cost_estimate=pl.CostEstimate(
            flops=2 * count * width * 2 * H + 4 * count * H * BLOCK_ROWS * half,
            bytes_accessed=4 * count * width,
            transcendentals=4 * count * H,
        ),
    )(tokens, query_weight, query_prior, head_t, proj)


def peer_kernel(
    tokens_ref, query_ref, prior_ref, map_ref, own_ref, legal_ref, label_ref, pool_ref, told_ref
):
    pool_into(pool_ref, tokens_ref, query_ref, prior_ref)
    tables = [map_ref[:SPREAD], map_ref[SPREAD:]]
    rows = own_ref.shape[2]
    told_ref[:PAD] = raw_sums(tables, [own_ref, pool_ref], 0)
    told_ref[PAD:] = jnp.zeros((PAD, 2 * rows), F32)
    told_ref[PAD : PAD + A, :rows] = legal_ref[...].astype(F32)
    told_ref[PAD + A : PAD + A + 1, :rows] = label_ref[...].astype(F32)


def peer_side(tokens, query_weight, query_prior, own_map, own_pool, legal_t, label):
    count, width = tokens.shape
    half = own_map.shape[1]
    return pl.pallas_call(
        peer_kernel,
        in_specs=[IN_VMEM] * 7,
        out_specs=[IN_VMEM] * 2,
        out_shape=[
            jax.ShapeDtypeStruct((2, H, count // OBS, half), BF16),
            jax.ShapeDtypeStruct((2 * PAD, 2 * count // OBS), F32),
        ],
        compiler_params=pltpu.CompilerParams(vmem_limit_bytes=PEER_MIB * MIB),
        cost_estimate=pl.CostEstimate(
            flops=2 * count * width * 2 * H + 4 * count * H * BLOCK_ROWS * half,
            bytes_accessed=2 * count * width + 2 * count * half,
            transcendentals=4 * count * H,
        ),
    )(tokens, query_weight, query_prior, own_map, own_pool, legal_t, label)


def finish_raw(top, rest):
    rest = rest[:8] + rest[8:]
    rest = rest + jnp.concatenate([rest[4:], rest[:4]], axis=0)
    return jnp.concatenate([top, rest], axis=0)


def raw_sums(tables, pools, which):
    rows = len(pools) * pools[0].shape[2]
    total = jnp.zeros((rows, 2 * TOP * len(tables)), F32)
    lane = lax.broadcasted_iota(jnp.int32, total.shape, 1) & (2 * TOP - 1)
    for h in range(H):
        right = []
        for table in tables:
            right += [table[h * TOP : (h + 1) * TOP], table[H * TOP + h // 4 * TOP :][:TOP]]
        pooled = jnp.concatenate([pool[which, h] for pool in pools], axis=0)
        result = dot_nt(pooled, jnp.concatenate(right, axis=0))
        kept = (lane < TOP) | ((lane - TOP) >> 2 == h % 4)
        total = total + jnp.where(kept, result, 0.0)
    total = total.T
    total = sum(total[2 * TOP * i :][: 2 * TOP] for i in range(len(tables)))
    return finish_raw(total[:TOP], total[TOP:])


def lower_kernel(map_ref, own_ref, peer_ref, earlier_ref, out_ref):
    level = lax.axis_index("dp") // PAIR

    @pl.when(level == 0)
    def _():
        out_ref[...] = jnp.zeros_like(out_ref)

    @pl.when(level > 0)
    def _():
        out_ref[...] = raw_sums([map_ref[...]], [own_ref, peer_ref], 1)


def lower_raw(lower_map, own_pool, peer_pool, earlier):
    _, _, rows, half = own_pool.shape
    return pl.pallas_call(
        lower_kernel,
        in_specs=[IN_VMEM] * 4,
        out_specs=IN_VMEM,
        out_shape=jax.ShapeDtypeStruct((PAD, 2 * rows), F32),
        compiler_params=pltpu.CompilerParams(vmem_limit_bytes=12 * MIB),
        cost_estimate=pl.CostEstimate(
            flops=8 * TOP * rows * H * half, bytes_accessed=4 * rows * H * half, transcendentals=0
        ),
    )(lower_map, own_pool, peer_pool, earlier)


def policy_rows(raws, legal):
    squashed = jnp.tanh(jnp.concatenate(raws, axis=0) * (1.0 / 30.0))
    logits = 30.0 * squashed
    exp_logits = jnp.exp(logits)
    found = []
    for i in range(len(raws)):
        rows = slice(i * PAD, (i + 1) * PAD)
        weights = exp_logits[rows] * legal
        partition = jnp.sum(weights, axis=0, keepdims=True)
        found.append((squashed[rows], logits[rows], weights * (1.0 / partition), partition))
    return found


def swapped(theirs):
    rows = theirs.shape[1] // 2
    return jnp.concatenate([theirs[:, rows:], theirs[:, :rows]], axis=1)


def grad_into(out_ref, loss_ref, out_buf, loss_buf, sems, mine_ref, theirs_ref, wide_ref, own_ref, peer_ref, lower):
    rows = own_ref.shape[2]
    told = jnp.concatenate([mine_ref[PAD:, :rows], theirs_ref[PAD:, :rows]], axis=1)
    move = lax.broadcasted_iota(jnp.int32, told.shape, 0)
    legal = jnp.where(move < A, told, 0.0)
    onehot = (move.astype(F32) == told[A : A + 1]).astype(F32)
    raws = [mine_ref[:PAD] + swapped(theirs_ref[:PAD])] + lower
    found = policy_rows(raws, legal)
    squashed, logits, policy, partition = found[0]
    if lower:
        partner = found[1][2]
    else:
        partner = legal * (1.0 / jnp.sum(legal, axis=0, keepdims=True))
    target = 0.5 * onehot + 0.5 * partner
    log_policy = logits - jnp.log(partition)
    loss = -jnp.sum(target * log_policy, axis=0, keepdims=True)
    loss_buf[...] = loss[:, :rows]
    loss_copy = pltpu.make_async_copy(loss_buf, loss_ref, sems.at[GRAD_CHUNKS])
    loss_copy.start()
    logit_grad = (policy - target) * (1.0 - squashed * squashed)
    high, low = split_high(logit_grad)
    left = jnp.concatenate([high.astype(F32), low.astype(F32)], axis=0).astype(BF16)
    chunk = out_buf.shape[0] // GRAD_CHUNKS
    copies = []
    for i in range(GRAD_CHUNKS):
        columns = slice(i * chunk, (i + 1) * chunk)
        narrow = []
        for h in range(H):
            pooled = jnp.concatenate([own_ref[0, h, :, columns], peer_ref[0, h, :, columns]], axis=0)
            product = dot_nn(left, pooled)
            narrow.append(product[:PAD] + product[PAD:])
        narrow = jnp.concatenate(narrow, axis=0).astype(BF16)
        out_buf[columns, :] = dot_tn(narrow, wide_ref[...])
        part = pl.ds(i * chunk, chunk)
        copies.append(pltpu.make_async_copy(out_buf.at[part], out_ref.at[part], sems.at[i]))
        copies[i].start()
    for copy in copies + [loss_copy]:
        copy.wait()


def lowest_grad_kernel(
    mine_ref, theirs_ref, wide_ref, own_ref, peer_ref,
    out_ref, loss_ref, token_ref, out_buf, loss_buf, sems,
):
    token_ref[...] = jnp.zeros_like(token_ref)

    @pl.when(lax.axis_index("dp") // PAIR == 0)
    def _():
        grad_into(
            out_ref, loss_ref, out_buf, loss_buf, sems,
            mine_ref, theirs_ref, wide_ref, own_ref, peer_ref, [],
        )


def upper_grad_kernel(
    mine_ref, theirs_ref, wide_ref, own_ref, peer_ref,
    lower_ref, lower_theirs_ref, lowest_ref, lowest_loss_ref,
    out_ref, loss_ref, out_buf, loss_buf, sems,
):
    @pl.when(lax.axis_index("dp") // PAIR > 0)
    def _():
        grad_into(
            out_ref, loss_ref, out_buf, loss_buf, sems,
            mine_ref, theirs_ref, wide_ref, own_ref, peer_ref,
            [lower_ref[...] + swapped(lower_theirs_ref[...])],
        )


def gradient(kernel, operands, into):
    _, _, rows, half = operands[3].shape
    width = H * DH
    count = len(operands)
    return pl.pallas_call(
        kernel,
        in_specs=[IN_VMEM] * count + [IN_HBM] * len(into),
        out_specs=[IN_HBM, IN_HBM] + ([] if into else [IN_VMEM]),
        out_shape=[
            jax.ShapeDtypeStruct((half, width), F32),
            jax.ShapeDtypeStruct((1, rows), F32),
        ]
        + ([] if into else [jax.ShapeDtypeStruct((8, DH), F32)]),
        input_output_aliases={count + i: i for i in range(len(into))},
        scratch_shapes=[
            pltpu.VMEM((half, width), F32),
            pltpu.VMEM((1, rows), F32),
            pltpu.SemaphoreType.DMA((GRAD_CHUNKS + 1,)),
        ],
        compiler_params=pltpu.CompilerParams(vmem_limit_bytes=16 * MIB),
        cost_estimate=pl.CostEstimate(
            flops=2 * H * PAD * half * width,
            bytes_accessed=4 * half * width + 4 * rows * H * half,
            transcendentals=0,
        ),
    )(*operands, *into)


def rotated(block, axis, distance):
    count = lax.axis_size(axis)
    return lax.ppermute(block, axis, [(i, (i + distance) % count) for i in range(count)])


def paired_device(
    tokens, legal_moves, action_label, value_weight, value_prior,
    query_weight, query_prior, policy_head, head_prior,
):
    peer_tokens = partner_2(tokens, "dp", 0)
    spread = head_spread(jnp.transpose(head_prior, (1, 0, 2)))
    prior_map = prior_fold(spread, value_prior)
    lower_map = rotated(prior_map, "dp", PAIR)
    own_pool, own_map, wide = own_side(
        tokens, query_weight, query_prior, jnp.transpose(policy_head, (1, 0, 2)), value_weight
    )
    peer_pool, mine = peer_side(
        peer_tokens, query_weight, query_prior, own_map, own_pool,
        legal_moves.T, action_label.reshape(1, -1),
    )
    theirs = partner_2(mine, "dp", 0)
    operands = [mine, theirs, wide, own_pool, peer_pool]
    *lowest, token = gradient(lowest_grad_kernel, operands, [])
    lower = lower_raw(lower_map, own_pool, peer_pool, token)
    lower_theirs = partner_2(lower, "dp", 0)
    weight_grad, row_loss = gradient(upper_grad_kernel, operands + [lower, lower_theirs], lowest)
    return weight_grad, row_loss.reshape(-1)


def solution(mesh):
    paired = mesh.shape["dp"] == LEVELS * PAIR
    return jax.shard_map(
        paired_device if paired else general_device,
        mesh=mesh,
        in_specs=(
            P(("groups", "dp"), None),
            P(("groups", "dp"), None),
            P(("groups", "dp")),
            P("dp", None),
            P("dp", None),
            P(),
            P(),
            P(),
            P(),
        ),
        out_specs=(P(("groups", "dp"), None), P(("groups", "dp"))),
        check_vma=False,
    )
```

```python
import jax
import jax.numpy as jnp
from jax import lax
from jax.experimental import pallas as pl
from jax.experimental.pallas import tpu as pltpu
from jax.sharding import PartitionSpec as P

H = 8
DH = 128
A = 20
OBS = 16
LEVELS = 8
EXACT = lax.Precision.HIGHEST


def partner_2(block, axis, bit):
    count = lax.axis_size(axis)
    route = []
    for low in range(count):
        high = low | 1 << bit
        if high != low and high < count:
            route += [(low, high), (high, low)]
    return lax.ppermute(block, axis, route)


def shifted(block, axis, distance):
    devices = range(lax.axis_size(axis))
    route = [(i - distance, i) for i in devices if i - distance in devices]
    return lax.ppermute(block, axis, route)


def head_map(proj, move_head):
    depth = proj.shape[0]
    product = jnp.einsum(
        "dhe,ahe->had",
        proj.astype(jnp.float32).reshape(depth, H, DH),
        move_head.reshape(A, H, DH),
        precision=EXACT,
    )
    return product.reshape(H * A, depth).astype(jnp.bfloat16)


def gather_columns(block, member, bit_count):
    for bit_place in range(bit_count):
        received = partner_2(block, "dp", bit_place)
        upper_side = member // (1 << bit_place) % 2 == 1
        lower_half = jnp.where(upper_side, received, block)
        upper_half = jnp.where(upper_side, block, received)
        block = jnp.concatenate([lower_half, upper_half], axis=1)
    return block


def scatter_columns(block, member, bit_count):
    for bit_place in reversed(range(bit_count)):
        half = block.shape[1] // 2
        upper_side = member // (1 << bit_place) % 2 == 1
        kept = jnp.where(upper_side, block[:, half:], block[:, :half])
        sent = jnp.where(upper_side, block[:, :half], block[:, half:])
        block = kept + partner_2(sent, "dp", bit_place)
    return block


def attention_of(tokens, query_proj):
    scores = lax.dot_general(
        tokens, query_proj, (((1,), (1,)), ((), ())), preferred_element_type=jnp.float32
    ).reshape(-1, OBS, H)
    exp_scores = jnp.exp(5.0 * jnp.tanh(scores / 5.0))
    attention = exp_scores / jnp.sum(exp_scores, axis=1, keepdims=True)
    return attention.astype(jnp.bfloat16).astype(jnp.float32)


def policy_of(tokens, attention, mapped, legal_float):
    row_count = legal_float.shape[0]
    moved = lax.dot_general(
        tokens, mapped, (((1,), (1,)), ((), ())), preferred_element_type=jnp.float32
    ).reshape(row_count, OBS, H, A)
    raw_logits = jnp.sum(attention[..., None] * moved, axis=(1, 2))
    logits = 30.0 * jnp.tanh(raw_logits / 30.0)
    exp_logits = jnp.exp(logits) * legal_float
    partition = jnp.sum(exp_logits, axis=1, keepdims=True)
    return logits, exp_logits / partition, logits - jnp.log(partition)


def general_device(
    tokens, legal_moves, action_label, value_weight, value_prior,
    query_weight, query_prior, policy_head, head_prior,
):
    group_size = lax.axis_size("dp") // LEVELS
    bit_count = group_size.bit_length() - 1
    device_place = lax.axis_index("dp")
    level_index = device_place // group_size
    member = device_place % group_size
    lower_index = jnp.maximum(level_index - 1, 0)

    def of_level(array, index):
        return lax.dynamic_index_in_dim(array, index, 0, keepdims=False)

    move_head = of_level(policy_head, level_index)
    prior_map = head_map(value_prior, of_level(head_prior, level_index))
    own_map = head_map(value_weight, move_head)
    lower_map = gather_columns(shifted(prior_map, "dp", group_size), member, bit_count)
    own_map = gather_columns(own_map, member, bit_count)
    attention = attention_of(tokens, of_level(query_weight, level_index))
    lower_attention = attention_of(tokens, of_level(query_prior, lower_index))
    legal_float = legal_moves.astype(jnp.float32)
    logits, policy, log_policy = policy_of(tokens, attention, own_map, legal_float)
    _, lower_policy, _ = policy_of(tokens, lower_attention, lower_map, legal_float)
    uniform_policy = legal_float / jnp.sum(legal_float, axis=1, keepdims=True)
    partner = jnp.where(level_index == 0, uniform_policy, lower_policy)
    onehot = (action_label[:, None] == jnp.arange(A, dtype=jnp.int32)[None, :]).astype(jnp.float32)
    target = 0.5 * onehot + 0.5 * partner
    row_loss = -jnp.sum(target * log_policy, axis=1)
    logit_grad = (policy - target) * (1.0 - (logits / 30.0) ** 2)
    token_grad = attention[..., None] * logit_grad[:, None, None, :]
    token_grad = token_grad.astype(jnp.bfloat16).reshape(tokens.shape[0], H * A)
    mapped_grad = lax.dot_general(
        token_grad, tokens, (((0,), (0,)), ((), ())), preferred_element_type=jnp.float32
    )
    mapped_grad = scatter_columns(mapped_grad, member, bit_count).reshape(H, A, -1)
    weight_grad = jnp.einsum(
        "had,ahe->dhe", mapped_grad, move_head.reshape(A, H, DH), precision=EXACT
    )
    return weight_grad.reshape(-1, H * DH), row_loss


PAIR = 2
TOP = 16
SPREAD = H * A
BLOCK_ROWS = 16
F32 = jnp.float32
BF16 = jnp.bfloat16
PAD = 24
PAIR_ROWS = 48
GRAD_CHUNKS = 4
DH_BITS = 7
OBS_BITS = 4
MIB = 2**20
PRIOR_MIB = 12
OWN_MIB = 16
PEER_MIB = 16
PRIOR_COST = 40
SPREAD_COST = 100000
SPREAD_MIB = 53.5


def dot_nt(left, right):
    return lax.dot_general(left, right, (((1,), (1,)), ((), ())), preferred_element_type=F32)


def dot_nn(left, right):
    return lax.dot_general(left, right, (((1,), (0,)), ((), ())), preferred_element_type=F32)


def dot_tn(left, right):
    return lax.dot_general(
        left, right, (((0,), (0,)), ((), ())), preferred_element_type=F32
    )


def split_high(value):
    high = value.astype(BF16)
    return high, (value - high.astype(F32)).astype(BF16)


def spread_heads(rows):
    width = 2 * DH
    lane_head = lax.broadcasted_iota(jnp.int32, (TOP, width), 1) >> DH_BITS
    upper = lax.broadcasted_iota(jnp.int32, (8, width), 0) >> 2
    pieces = []
    for pair in range(H // 2):
        part = rows[:, pair * width : (pair + 1) * width]
        rest = jnp.concatenate([part[TOP:A], part[TOP:A]], axis=0)
        pieces += [
            jnp.where(lane_head == 0, part[:TOP], 0.0),
            jnp.where(lane_head == 1, part[:TOP], 0.0),
            jnp.where(lane_head[:8] == upper, rest, 0.0),
            jnp.zeros((8, width), F32),
        ]
    return jnp.concatenate(pieces, axis=0)


def level_head(head_ref):
    level = lax.axis_index("dp") // PAIR
    return head_ref[:, pl.ds(level, 1), :].reshape(A, H * DH)


def spread_into(spread_ref, head):
    high, low = split_high(spread_heads(head))
    for pair in range(H // 2):
        at = 2 * pair * PAIR_ROWS
        rows = slice(pair * PAIR_ROWS, (pair + 1) * PAIR_ROWS)
        spread_ref[at : at + PAIR_ROWS, :] = high[rows]
        spread_ref[at + PAIR_ROWS : at + 2 * PAIR_ROWS, :] = low[rows]


def fold_into(out_ref, proj_ref, spread_ref, parts):
    tops, rests = [], []
    for pair in range(H // 2):
        proj = proj_ref[:, pair * 2 * DH : (pair + 1) * 2 * DH]
        spread = spread_ref[2 * pair * PAIR_ROWS : 2 * (pair + 1) * PAIR_ROWS]
        product = dot_nt(proj, spread).T
        product = product[:PAIR_ROWS] + product[PAIR_ROWS:]
        tops.append(product[: 2 * TOP])
        rests.append(product[2 * TOP : 2 * TOP + 8])
    product = jnp.concatenate(tops + rests, axis=0)
    if parts == 1:
        out_ref[...] = product.astype(BF16)
    else:
        high, low = split_high(product)
        out_ref[:SPREAD] = high
        out_ref[SPREAD:] = low


def spread_kernel(head_ref, spread_ref, head_buf, sem):
    level = lax.axis_index("dp") // PAIR
    copy = pltpu.make_async_copy(head_ref.at[:, pl.ds(level, 1)], head_buf, sem)
    copy.start()
    copy.wait()
    spread_into(spread_ref, head_buf[...].reshape(A, H * DH))


def prior_kernel(spread_ref, proj_ref, out_ref):
    fold_into(out_ref, proj_ref, spread_ref, 1)


IN_HBM = pl.BlockSpec(memory_space=pltpu.HBM)
IN_VMEM = pl.BlockSpec(memory_space=pltpu.VMEM)


def head_spread(head_t):
    width = head_t.shape[2]
    return pl.pallas_call(
        spread_kernel,
        in_specs=[IN_HBM],
        out_specs=IN_VMEM,
        out_shape=jax.ShapeDtypeStruct((H * PAIR_ROWS, 2 * DH), BF16),
        scratch_shapes=[pltpu.VMEM((A, 1, width), F32), pltpu.SemaphoreType.DMA],
        compiler_params=pltpu.CompilerParams(vmem_limit_bytes=int(SPREAD_MIB * MIB)),
        cost_estimate=pl.CostEstimate(
            flops=SPREAD_COST * SPREAD * width, bytes_accessed=4 * head_t.size, transcendentals=0
        ),
    )(head_t)


def prior_fold(spread, proj):
    depth, width = proj.shape
    return pl.pallas_call(
        prior_kernel,
        in_specs=[IN_VMEM, IN_VMEM],
        out_specs=IN_VMEM,
        out_shape=jax.ShapeDtypeStruct((SPREAD, depth), BF16),
        compiler_params=pltpu.CompilerParams(vmem_limit_bytes=PRIOR_MIB * MIB),
        cost_estimate=pl.CostEstimate(
            flops=PRIOR_COST * SPREAD * depth * width,
            bytes_accessed=2 * depth * width,
            transcendentals=0,
        ),
    )(spread, proj)


def pool_into(out_ref, tokens_ref, query_ref, prior_ref):
    count = tokens_ref.shape[0]
    half = out_ref.shape[3]
    block = BLOCK_ROWS * OBS
    blocks = count // block
    device_place = lax.axis_index("dp")
    level = device_place // PAIR
    lower = jnp.maximum(level - 1, 0)
    queries = jnp.concatenate(
        [query_ref[level].astype(F32), prior_ref[lower].astype(F32)], axis=0
    ).astype(BF16)
    row_of = lax.broadcasted_iota(jnp.int32, (block, block), 0) >> OBS_BITS
    column_of = lax.broadcasted_iota(jnp.int32, (block, block), 1) >> OBS_BITS
    same_row = (row_of == column_of).astype(F32).astype(BF16)
    mask = (
        lax.broadcasted_iota(jnp.int32, (BLOCK_ROWS, block), 0)
        == lax.broadcasted_iota(jnp.int32, (BLOCK_ROWS, block), 1) >> OBS_BITS
    )
    start = pl.multiple_of(device_place % PAIR * half, half)
    scores = dot_nt(queries, tokens_ref[...])
    scores = [scores[:, i * block : (i + 1) * block] for i in range(blocks)]
    exp_scores = jnp.exp(5.0 * jnp.tanh(jnp.concatenate(scores, axis=0) / 5.0))
    first, rest = split_high(exp_scores)
    second, third = split_high(exp_scores - first.astype(F32))
    parts = dot_nn(jnp.concatenate([first, second, third], axis=0), same_row)
    rows = 2 * H * blocks
    total = parts[:rows] + parts[rows : 2 * rows] + parts[2 * rows :]
    attention = (exp_scores / total).astype(BF16).astype(F32)
    for i in range(blocks):
        at = 2 * H * i
        spread = jnp.concatenate(
            [jnp.where(mask, attention[at + j : at + j + 1], 0.0) for j in range(2 * H)], axis=0
        ).astype(BF16)
        pooled = dot_nn(spread, tokens_ref[i * block : (i + 1) * block, pl.ds(start, half)])
        out_ref[:, :, i * BLOCK_ROWS : (i + 1) * BLOCK_ROWS, :] = pooled.astype(BF16).reshape(
            2, H, BLOCK_ROWS, half
        )


def own_kernel(
    tokens_ref, query_ref, prior_ref, head_ref, proj_ref, pool_ref, map_ref, wide_ref, spread_ref
):
    head = level_head(head_ref)
    spread_into(spread_ref, head)
    fold_into(map_ref, proj_ref, spread_ref, 2)
    empty = jnp.zeros((PAD - A, H * DH), F32)
    wide_ref[...] = jnp.concatenate([head, empty, head, empty], axis=0).astype(BF16)
    pool_into(pool_ref, tokens_ref, query_ref, prior_ref)


def own_side(tokens, query_weight, query_prior, head_t, proj):
    count, width = tokens.shape
    half = proj.shape[0]
    return pl.pallas_call(
        own_kernel,
        in_specs=[IN_VMEM] * 5,
        out_specs=[IN_VMEM] * 3,
        out_shape=[
            jax.ShapeDtypeStruct((2, H, count // OBS, half), BF16),
            jax.ShapeDtypeStruct((2 * SPREAD, half), BF16),
            jax.ShapeDtypeStruct((2 * PAD, H * DH), BF16),
        ],
        scratch_shapes=[pltpu.VMEM((H * PAIR_ROWS, 2 * DH), BF16)],
        compiler_params=pltpu.CompilerParams(vmem_limit_bytes=OWN_MIB * MIB),
        cost_estimate=pl.CostEstimate(
            flops=2 * count * width * 2 * H + 4 * count * H * BLOCK_ROWS * half,
            bytes_accessed=4 * count * width,
            transcendentals=4 * count * H,
        ),
    )(tokens, query_weight, query_prior, head_t, proj)


def peer_kernel(
    tokens_ref, query_ref, prior_ref, map_ref, own_ref, legal_ref, label_ref,
    pool_ref, told_ref, turned_ref,
):
    pool_into(pool_ref, tokens_ref, query_ref, prior_ref)
    tables = [map_ref[:SPREAD], map_ref[SPREAD:]]
    rows = own_ref.shape[2]
    told_ref[:PAD] = raw_sums(tables, [own_ref, pool_ref], 0)
    told_ref[PAD:] = jnp.zeros((PAD, 2 * rows), F32)
    told_ref[PAD : PAD + A, :rows] = legal_ref[...].astype(F32)
    told_ref[PAD + A : PAD + A + 1, :rows] = label_ref[...].astype(F32)
    for h in range(H):
        pooled = jnp.concatenate([own_ref[0, h], pool_ref[0, h]], axis=0)
        turned_ref[:, h * 2 * rows : (h + 1) * 2 * rows] = pooled.T


def peer_side(tokens, query_weight, query_prior, own_map, own_pool, legal_t, label):
    count, width = tokens.shape
    half = own_map.shape[1]
    return pl.pallas_call(
        peer_kernel,
        in_specs=[IN_VMEM] * 7,
        out_specs=[IN_VMEM] * 3,
        out_shape=[
            jax.ShapeDtypeStruct((2, H, count // OBS, half), BF16),
            jax.ShapeDtypeStruct((2 * PAD, 2 * count // OBS), F32),
            jax.ShapeDtypeStruct((half, 2 * H * count // OBS), BF16),
        ],
        compiler_params=pltpu.CompilerParams(vmem_limit_bytes=PEER_MIB * MIB),
        cost_estimate=pl.CostEstimate(
            flops=2 * count * width * 2 * H + 4 * count * H * BLOCK_ROWS * half,
            bytes_accessed=2 * count * width + 2 * count * half,
            transcendentals=4 * count * H,
        ),
    )(tokens, query_weight, query_prior, own_map, own_pool, legal_t, label)


def finish_raw(top, rest):
    rest = rest[:8] + rest[8:]
    rest = rest + jnp.concatenate([rest[4:], rest[:4]], axis=0)
    return jnp.concatenate([top, rest], axis=0)


def raw_sums(tables, pools, which):
    rows = len(pools) * pools[0].shape[2]
    total = jnp.zeros((rows, 2 * TOP * len(tables)), F32)
    lane = lax.broadcasted_iota(jnp.int32, total.shape, 1) & (2 * TOP - 1)
    for h in range(H):
        right = []
        for table in tables:
            right += [table[h * TOP : (h + 1) * TOP], table[H * TOP + h // 4 * TOP :][:TOP]]
        pooled = jnp.concatenate([pool[which, h] for pool in pools], axis=0)
        result = dot_nt(pooled, jnp.concatenate(right, axis=0))
        kept = (lane < TOP) | ((lane - TOP) >> 2 == h % 4)
        total = total + jnp.where(kept, result, 0.0)
    total = total.T
    total = sum(total[2 * TOP * i :][: 2 * TOP] for i in range(len(tables)))
    return finish_raw(total[:TOP], total[TOP:])


def lower_kernel(map_ref, own_ref, peer_ref, earlier_ref, out_ref):
    level = lax.axis_index("dp") // PAIR

    @pl.when(level == 0)
    def _():
        out_ref[...] = jnp.zeros_like(out_ref)

    @pl.when(level > 0)
    def _():
        out_ref[...] = raw_sums([map_ref[...]], [own_ref, peer_ref], 1)


def lower_raw(lower_map, own_pool, peer_pool, earlier):
    _, _, rows, half = own_pool.shape
    return pl.pallas_call(
        lower_kernel,
        in_specs=[IN_VMEM] * 4,
        out_specs=IN_VMEM,
        out_shape=jax.ShapeDtypeStruct((PAD, 2 * rows), F32),
        compiler_params=pltpu.CompilerParams(vmem_limit_bytes=12 * MIB),
        cost_estimate=pl.CostEstimate(
            flops=8 * TOP * rows * H * half, bytes_accessed=4 * rows * H * half, transcendentals=0
        ),
    )(lower_map, own_pool, peer_pool, earlier)


def policy_rows(raws, legal):
    squashed = jnp.tanh(jnp.concatenate(raws, axis=0) * (1.0 / 30.0))
    logits = 30.0 * squashed
    exp_logits = jnp.exp(logits)
    found = []
    for i in range(len(raws)):
        rows = slice(i * PAD, (i + 1) * PAD)
        weights = exp_logits[rows] * legal
        partition = jnp.sum(weights, axis=0, keepdims=True)
        found.append((squashed[rows], logits[rows], weights * (1.0 / partition), partition))
    return found


def swapped(theirs):
    rows = theirs.shape[1] // 2
    return jnp.concatenate([theirs[:, rows:], theirs[:, :rows]], axis=1)


def grad_into(out_ref, loss_ref, out_buf, loss_buf, sems, mine_ref, theirs_ref, wide_ref, turned_ref, lower):

    rows = mine_ref.shape[1] // 2
    told = jnp.concatenate([mine_ref[PAD:, :rows], theirs_ref[PAD:, :rows]], axis=1)
    move = lax.broadcasted_iota(jnp.int32, told.shape, 0)
    legal = jnp.where(move < A, told, 0.0)
    onehot = (move.astype(F32) == told[A : A + 1]).astype(F32)
    raws = [mine_ref[:PAD] + swapped(theirs_ref[:PAD])] + lower
    found = policy_rows(raws, legal)
    squashed, logits, policy, partition = found[0]
    if lower:
        partner = found[1][2]
    else:
        partner = legal * (1.0 / jnp.sum(legal, axis=0, keepdims=True))
    target = 0.5 * onehot + 0.5 * partner
    log_policy = logits - jnp.log(partition)
    loss = -jnp.sum(target * log_policy, axis=0, keepdims=True)
    loss_buf[...] = loss[:, :rows]
    loss_copy = pltpu.make_async_copy(loss_buf, loss_ref, sems.at[GRAD_CHUNKS])
    loss_copy.start()
    logit_grad = (policy - target) * (1.0 - squashed * squashed)
    high, low = split_high(logit_grad)
    left = jnp.concatenate([high.astype(F32), low.astype(F32)], axis=0).astype(BF16)
    pooled_grad = dot_tn(left, wide_ref[...]).astype(BF16)
    empty = jnp.zeros((2 * rows, DH), BF16)
    diagonal = []
    for pair in range(H // 2):
        first = pooled_grad[:, 2 * pair * DH : (2 * pair + 1) * DH]
        second = pooled_grad[:, (2 * pair + 1) * DH : 2 * (pair + 1) * DH]
        first = jnp.concatenate([first, empty], axis=1)
        second = jnp.concatenate([empty, second], axis=1)
        diagonal.append(jnp.concatenate([first, second], axis=0))
    chunk = out_buf.shape[0] // GRAD_CHUNKS
    copies = []
    for i in range(GRAD_CHUNKS):
        for pair in range(H // 2):
            turned = turned_ref[
                i * chunk : (i + 1) * chunk, 4 * pair * rows : 4 * (pair + 1) * rows
            ]
            out_buf[i * chunk : (i + 1) * chunk, 2 * pair * DH : 2 * (pair + 1) * DH] = dot_nn(
                turned, diagonal[pair]
            )
        part = pl.ds(i * chunk, chunk)
        copies.append(pltpu.make_async_copy(out_buf.at[part], out_ref.at[part], sems.at[i]))
        copies[i].start()
    for copy in copies + [loss_copy]:
        copy.wait()


def lowest_grad_kernel(
    mine_ref, theirs_ref, wide_ref, turned_ref,
    out_ref, loss_ref, token_ref, out_buf, loss_buf, sems,
):
    token_ref[...] = jnp.zeros_like(token_ref)

    @pl.when(lax.axis_index("dp") // PAIR == 0)
    def _():
        grad_into(
            out_ref, loss_ref, out_buf, loss_buf, sems,
            mine_ref, theirs_ref, wide_ref, turned_ref, [],
        )


def upper_grad_kernel(
    mine_ref, theirs_ref, wide_ref, turned_ref,
    lower_ref, lower_theirs_ref, lowest_ref, lowest_loss_ref,
    out_ref, loss_ref, out_buf, loss_buf, sems,
):
    @pl.when(lax.axis_index("dp") // PAIR > 0)
    def _():
        grad_into(
            out_ref, loss_ref, out_buf, loss_buf, sems,
            mine_ref, theirs_ref, wide_ref, turned_ref,
            [lower_ref[...] + swapped(lower_theirs_ref[...])],
        )


def gradient(kernel, operands, into):
    half = operands[3].shape[0]
    rows = operands[0].shape[1] // 2
    width = H * DH
    count = len(operands)
    return pl.pallas_call(
        kernel,
        in_specs=[IN_VMEM] * count + [IN_HBM] * len(into),
        out_specs=[IN_HBM, IN_HBM] + ([] if into else [IN_VMEM]),
        out_shape=[
            jax.ShapeDtypeStruct((half, width), F32),
            jax.ShapeDtypeStruct((1, rows), F32),
        ]
        + ([] if into else [jax.ShapeDtypeStruct((8, DH), F32)]),
        input_output_aliases={count + i: i for i in range(len(into))},
        scratch_shapes=[
            pltpu.VMEM((half, width), F32),
            pltpu.VMEM((1, rows), F32),
            pltpu.SemaphoreType.DMA((GRAD_CHUNKS + 1,)),
        ],
        compiler_params=pltpu.CompilerParams(vmem_limit_bytes=16 * MIB),
        cost_estimate=pl.CostEstimate(
            flops=2 * H * PAD * half * width,
            bytes_accessed=4 * half * width + 4 * rows * H * half,
            transcendentals=0,
        ),
    )(*operands, *into)


def rotated(block, axis, distance):
    count = lax.axis_size(axis)
    return lax.ppermute(block, axis, [(i, (i + distance) % count) for i in range(count)])


def paired_device(
    tokens, legal_moves, action_label, value_weight, value_prior,
    query_weight, query_prior, policy_head, head_prior,
):
    peer_tokens = partner_2(tokens, "dp", 0)
    spread = head_spread(jnp.transpose(head_prior, (1, 0, 2)))
    prior_map = prior_fold(spread, value_prior)
    lower_map = rotated(prior_map, "dp", PAIR)
    own_pool, own_map, wide = own_side(
        tokens, query_weight, query_prior, jnp.transpose(policy_head, (1, 0, 2)), value_weight
    )
    peer_pool, mine, turned = peer_side(
        peer_tokens, query_weight, query_prior, own_map, own_pool,
        legal_moves.T, action_label.reshape(1, -1),
    )
    theirs = partner_2(mine, "dp", 0)
    operands = [mine, theirs, wide, turned]
    *lowest, token = gradient(lowest_grad_kernel, operands, [])
    lower = lower_raw(lower_map, own_pool, peer_pool, token)
    lower_theirs = partner_2(lower, "dp", 0)
    weight_grad, row_loss = gradient(upper_grad_kernel, operands + [lower, lower_theirs], lowest)
    return weight_grad, row_loss.reshape(-1)


def solution(mesh):
    paired = mesh.shape["dp"] == LEVELS * PAIR
    return jax.shard_map(
        paired_device if paired else general_device,
        mesh=mesh,
        in_specs=(
            P(("groups", "dp"), None),
            P(("groups", "dp"), None),
            P(("groups", "dp")),
            P("dp", None),
            P("dp", None),
            P(),
            P(),
            P(),
            P(),
        ),
        out_specs=(P(("groups", "dp"), None), P(("groups", "dp"))),
        check_vma=False,
    )
```

```python
import jax
import jax.numpy as jnp
from jax import lax
from jax.experimental import pallas as pl
from jax.experimental.pallas import tpu as pltpu
from jax.sharding import PartitionSpec as P

H = 8
DH = 128
A = 20
OBS = 16
LEVELS = 8
EXACT = lax.Precision.HIGHEST


def partner_2(block, axis, bit):
    count = lax.axis_size(axis)
    route = []
    for low in range(count):
        high = low | 1 << bit
        if high != low and high < count:
            route += [(low, high), (high, low)]
    return lax.ppermute(block, axis, route)


def shifted(block, axis, distance):
    devices = range(lax.axis_size(axis))
    route = [(i - distance, i) for i in devices if i - distance in devices]
    return lax.ppermute(block, axis, route)


def head_map(proj, move_head):
    depth = proj.shape[0]
    product = jnp.einsum(
        "dhe,ahe->had",
        proj.astype(jnp.float32).reshape(depth, H, DH),
        move_head.reshape(A, H, DH),
        precision=EXACT,
    )
    return product.reshape(H * A, depth).astype(jnp.bfloat16)


def gather_columns(block, member, bit_count):
    for bit_place in range(bit_count):
        received = partner_2(block, "dp", bit_place)
        upper_side = member // (1 << bit_place) % 2 == 1
        lower_half = jnp.where(upper_side, received, block)
        upper_half = jnp.where(upper_side, block, received)
        block = jnp.concatenate([lower_half, upper_half], axis=1)
    return block


def scatter_columns(block, member, bit_count):
    for bit_place in reversed(range(bit_count)):
        half = block.shape[1] // 2
        upper_side = member // (1 << bit_place) % 2 == 1
        kept = jnp.where(upper_side, block[:, half:], block[:, :half])
        sent = jnp.where(upper_side, block[:, :half], block[:, half:])
        block = kept + partner_2(sent, "dp", bit_place)
    return block


def attention_of(tokens, query_proj):
    scores = lax.dot_general(
        tokens, query_proj, (((1,), (1,)), ((), ())), preferred_element_type=jnp.float32
    ).reshape(-1, OBS, H)
    exp_scores = jnp.exp(5.0 * jnp.tanh(scores / 5.0))
    attention = exp_scores / jnp.sum(exp_scores, axis=1, keepdims=True)
    return attention.astype(jnp.bfloat16).astype(jnp.float32)


def policy_of(tokens, attention, mapped, legal_float):
    row_count = legal_float.shape[0]
    moved = lax.dot_general(
        tokens, mapped, (((1,), (1,)), ((), ())), preferred_element_type=jnp.float32
    ).reshape(row_count, OBS, H, A)
    raw_logits = jnp.sum(attention[..., None] * moved, axis=(1, 2))
    logits = 30.0 * jnp.tanh(raw_logits / 30.0)
    exp_logits = jnp.exp(logits) * legal_float
    partition = jnp.sum(exp_logits, axis=1, keepdims=True)
    return logits, exp_logits / partition, logits - jnp.log(partition)


def general_device(
    tokens, legal_moves, action_label, value_weight, value_prior,
    query_weight, query_prior, policy_head, head_prior,
):
    group_size = lax.axis_size("dp") // LEVELS
    bit_count = group_size.bit_length() - 1
    device_place = lax.axis_index("dp")
    level_index = device_place // group_size
    member = device_place % group_size
    lower_index = jnp.maximum(level_index - 1, 0)

    def of_level(array, index):
        return lax.dynamic_index_in_dim(array, index, 0, keepdims=False)

    move_head = of_level(policy_head, level_index)
    prior_map = head_map(value_prior, of_level(head_prior, level_index))
    own_map = head_map(value_weight, move_head)
    lower_map = gather_columns(shifted(prior_map, "dp", group_size), member, bit_count)
    own_map = gather_columns(own_map, member, bit_count)
    attention = attention_of(tokens, of_level(query_weight, level_index))
    lower_attention = attention_of(tokens, of_level(query_prior, lower_index))
    legal_float = legal_moves.astype(jnp.float32)
    logits, policy, log_policy = policy_of(tokens, attention, own_map, legal_float)
    _, lower_policy, _ = policy_of(tokens, lower_attention, lower_map, legal_float)
    uniform_policy = legal_float / jnp.sum(legal_float, axis=1, keepdims=True)
    partner = jnp.where(level_index == 0, uniform_policy, lower_policy)
    onehot = (action_label[:, None] == jnp.arange(A, dtype=jnp.int32)[None, :]).astype(jnp.float32)
    target = 0.5 * onehot + 0.5 * partner
    row_loss = -jnp.sum(target * log_policy, axis=1)
    logit_grad = (policy - target) * (1.0 - (logits / 30.0) ** 2)
    token_grad = attention[..., None] * logit_grad[:, None, None, :]
    token_grad = token_grad.astype(jnp.bfloat16).reshape(tokens.shape[0], H * A)
    mapped_grad = lax.dot_general(
        token_grad, tokens, (((0,), (0,)), ((), ())), preferred_element_type=jnp.float32
    )
    mapped_grad = scatter_columns(mapped_grad, member, bit_count).reshape(H, A, -1)
    weight_grad = jnp.einsum(
        "had,ahe->dhe", mapped_grad, move_head.reshape(A, H, DH), precision=EXACT
    )
    return weight_grad.reshape(-1, H * DH), row_loss


PAIR = 2
TOP = 16
SPREAD = H * A
BLOCK_ROWS = 16
F32 = jnp.float32
BF16 = jnp.bfloat16
PAD = 24
PAIR_ROWS = 48
GRAD_CUTS = (0, 1, 2, 4, 6, 8)
GRAD_UNITS = GRAD_CUTS[-1]
GRAD_CHUNKS = len(GRAD_CUTS) - 1
DH_BITS = 7
OBS_BITS = 4
MIB = 2**20
PRIOR_MIB = 12
OWN_MIB = 16
PEER_MIB = 16
PRIOR_COST = 40
SPREAD_COST = 100000
SPREAD_MIB = 53.5


def dot_nt(left, right):
    return lax.dot_general(left, right, (((1,), (1,)), ((), ())), preferred_element_type=F32)


def dot_nn(left, right):
    return lax.dot_general(left, right, (((1,), (0,)), ((), ())), preferred_element_type=F32)


def dot_tn(left, right):
    return lax.dot_general(
        left, right, (((0,), (0,)), ((), ())), preferred_element_type=F32
    )


def split_high(value):
    high = value.astype(BF16)
    return high, (value - high.astype(F32)).astype(BF16)


def spread_heads(rows):
    width = 2 * DH
    lane_head = lax.broadcasted_iota(jnp.int32, (TOP, width), 1) >> DH_BITS
    upper = lax.broadcasted_iota(jnp.int32, (8, width), 0) >> 2
    pieces = []
    for pair in range(H // 2):
        part = rows[:, pair * width : (pair + 1) * width]
        rest = jnp.concatenate([part[TOP:A], part[TOP:A]], axis=0)
        pieces += [
            jnp.where(lane_head == 0, part[:TOP], 0.0),
            jnp.where(lane_head == 1, part[:TOP], 0.0),
            jnp.where(lane_head[:8] == upper, rest, 0.0),
            jnp.zeros((8, width), F32),
        ]
    return jnp.concatenate(pieces, axis=0)


def level_head(head_ref):
    level = lax.axis_index("dp") // PAIR
    return head_ref[:, pl.ds(level, 1), :].reshape(A, H * DH)


def spread_into(spread_ref, head):
    high, low = split_high(spread_heads(head))
    for pair in range(H // 2):
        at = 2 * pair * PAIR_ROWS
        rows = slice(pair * PAIR_ROWS, (pair + 1) * PAIR_ROWS)
        spread_ref[at : at + PAIR_ROWS, :] = high[rows]
        spread_ref[at + PAIR_ROWS : at + 2 * PAIR_ROWS, :] = low[rows]


def fold_into(out_ref, proj_ref, spread_ref, parts):
    tops, rests = [], []
    for pair in range(H // 2):
        proj = proj_ref[:, pair * 2 * DH : (pair + 1) * 2 * DH]
        spread = spread_ref[2 * pair * PAIR_ROWS : 2 * (pair + 1) * PAIR_ROWS]
        product = dot_nt(proj, spread).T
        product = product[:PAIR_ROWS] + product[PAIR_ROWS:]
        tops.append(product[: 2 * TOP])
        rests.append(product[2 * TOP : 2 * TOP + 8])
    product = jnp.concatenate(tops + rests, axis=0)
    if parts == 1:
        out_ref[...] = product.astype(BF16)
    else:
        high, low = split_high(product)
        out_ref[:SPREAD] = high
        out_ref[SPREAD:] = low


def spread_kernel(head_ref, spread_ref, head_buf, sem):
    level = lax.axis_index("dp") // PAIR
    copy = pltpu.make_async_copy(head_ref.at[:, pl.ds(level, 1)], head_buf, sem)
    copy.start()
    copy.wait()
    spread_into(spread_ref, head_buf[...].reshape(A, H * DH))


def prior_kernel(spread_ref, proj_ref, out_ref):
    fold_into(out_ref, proj_ref, spread_ref, 1)


IN_HBM = pl.BlockSpec(memory_space=pltpu.HBM)
IN_VMEM = pl.BlockSpec(memory_space=pltpu.VMEM)


def head_spread(head_t):
    width = head_t.shape[2]
    return pl.pallas_call(
        spread_kernel,
        in_specs=[IN_HBM],
        out_specs=IN_VMEM,
        out_shape=jax.ShapeDtypeStruct((H * PAIR_ROWS, 2 * DH), BF16),
        scratch_shapes=[pltpu.VMEM((A, 1, width), F32), pltpu.SemaphoreType.DMA],
        compiler_params=pltpu.CompilerParams(vmem_limit_bytes=int(SPREAD_MIB * MIB)),
        cost_estimate=pl.CostEstimate(
            flops=SPREAD_COST * SPREAD * width, bytes_accessed=4 * head_t.size, transcendentals=0
        ),
    )(head_t)


def prior_fold(spread, proj):
    depth, width = proj.shape
    return pl.pallas_call(
        prior_kernel,
        in_specs=[IN_VMEM, IN_VMEM],
        out_specs=IN_VMEM,
        out_shape=jax.ShapeDtypeStruct((SPREAD, depth), BF16),
        compiler_params=pltpu.CompilerParams(vmem_limit_bytes=PRIOR_MIB * MIB),
        cost_estimate=pl.CostEstimate(
            flops=PRIOR_COST * SPREAD * depth * width,
            bytes_accessed=2 * depth * width,
            transcendentals=0,
        ),
    )(spread, proj)


def pool_into(out_ref, tokens_ref, query_ref, prior_ref):
    count = tokens_ref.shape[0]
    half = out_ref.shape[3]
    block = BLOCK_ROWS * OBS
    blocks = count // block
    device_place = lax.axis_index("dp")
    level = device_place // PAIR
    lower = jnp.maximum(level - 1, 0)
    queries = jnp.concatenate(
        [query_ref[level].astype(F32), prior_ref[lower].astype(F32)], axis=0
    ).astype(BF16)
    row_of = lax.broadcasted_iota(jnp.int32, (block, block), 0) >> OBS_BITS
    column_of = lax.broadcasted_iota(jnp.int32, (block, block), 1) >> OBS_BITS
    same_row = (row_of == column_of).astype(F32).astype(BF16)
    mask = (
        lax.broadcasted_iota(jnp.int32, (BLOCK_ROWS, block), 0)
        == lax.broadcasted_iota(jnp.int32, (BLOCK_ROWS, block), 1) >> OBS_BITS
    )
    start = pl.multiple_of(device_place % PAIR * half, half)
    scores = dot_nt(queries, tokens_ref[...])
    scores = [scores[:, i * block : (i + 1) * block] for i in range(blocks)]
    exp_scores = jnp.exp(5.0 * jnp.tanh(jnp.concatenate(scores, axis=0) / 5.0))
    first, rest = split_high(exp_scores)
    second, third = split_high(exp_scores - first.astype(F32))
    parts = dot_nn(jnp.concatenate([first, second, third], axis=0), same_row)
    rows = 2 * H * blocks
    total = parts[:rows] + parts[rows : 2 * rows] + parts[2 * rows :]
    attention = (exp_scores / total).astype(BF16).astype(F32)
    for i in range(blocks):
        at = 2 * H * i
        spread = jnp.concatenate(
            [jnp.where(mask, attention[at + j : at + j + 1], 0.0) for j in range(2 * H)], axis=0
        ).astype(BF16)
        pooled = dot_nn(spread, tokens_ref[i * block : (i + 1) * block, pl.ds(start, half)])
        out_ref[:, :, i * BLOCK_ROWS : (i + 1) * BLOCK_ROWS, :] = pooled.astype(BF16).reshape(
            2, H, BLOCK_ROWS, half
        )


def own_kernel(
    tokens_ref, query_ref, prior_ref, head_ref, proj_ref, pool_ref, map_ref, wide_ref, spread_ref
):
    head = level_head(head_ref)
    spread_into(spread_ref, head)
    fold_into(map_ref, proj_ref, spread_ref, 2)
    empty = jnp.zeros((PAD - A, H * DH), F32)
    wide_ref[...] = jnp.concatenate([head, empty, head, empty], axis=0).astype(BF16)
    pool_into(pool_ref, tokens_ref, query_ref, prior_ref)


def own_side(tokens, query_weight, query_prior, head_t, proj):
    count, width = tokens.shape
    half = proj.shape[0]
    return pl.pallas_call(
        own_kernel,
        in_specs=[IN_VMEM] * 5,
        out_specs=[IN_VMEM] * 3,
        out_shape=[
            jax.ShapeDtypeStruct((2, H, count // OBS, half), BF16),
            jax.ShapeDtypeStruct((2 * SPREAD, half), BF16),
            jax.ShapeDtypeStruct((2 * PAD, H * DH), BF16),
        ],
        scratch_shapes=[pltpu.VMEM((H * PAIR_ROWS, 2 * DH), BF16)],
        compiler_params=pltpu.CompilerParams(vmem_limit_bytes=OWN_MIB * MIB),
        cost_estimate=pl.CostEstimate(
            flops=2 * count * width * 2 * H + 4 * count * H * BLOCK_ROWS * half,
            bytes_accessed=4 * count * width,
            transcendentals=4 * count * H,
        ),
    )(tokens, query_weight, query_prior, head_t, proj)


def peer_kernel(
    tokens_ref, query_ref, prior_ref, map_ref, own_ref, legal_ref, label_ref,
    pool_ref, told_ref, turned_ref,
):
    pool_into(pool_ref, tokens_ref, query_ref, prior_ref)
    tables = [map_ref[:SPREAD], map_ref[SPREAD:]]
    rows = own_ref.shape[2]
    told_ref[:PAD] = raw_sums(tables, [own_ref, pool_ref], 0)
    told_ref[PAD:] = jnp.zeros((PAD, 2 * rows), F32)
    told_ref[PAD : PAD + A, :rows] = legal_ref[...].astype(F32)
    told_ref[PAD + A : PAD + A + 1, :rows] = label_ref[...].astype(F32)
    for h in range(H):
        pooled = jnp.concatenate([own_ref[0, h], pool_ref[0, h]], axis=0)
        turned_ref[:, h * 2 * rows : (h + 1) * 2 * rows] = pooled.T


def peer_side(tokens, query_weight, query_prior, own_map, own_pool, legal_t, label):
    count, width = tokens.shape
    half = own_map.shape[1]
    return pl.pallas_call(
        peer_kernel,
        in_specs=[IN_VMEM] * 7,
        out_specs=[IN_VMEM] * 3,
        out_shape=[
            jax.ShapeDtypeStruct((2, H, count // OBS, half), BF16),
            jax.ShapeDtypeStruct((2 * PAD, 2 * count // OBS), F32),
            jax.ShapeDtypeStruct((half, 2 * H * count // OBS), BF16),
        ],
        compiler_params=pltpu.CompilerParams(vmem_limit_bytes=PEER_MIB * MIB),
        cost_estimate=pl.CostEstimate(
            flops=2 * count * width * 2 * H + 4 * count * H * BLOCK_ROWS * half,
            bytes_accessed=2 * count * width + 2 * count * half,
            transcendentals=4 * count * H,
        ),
    )(tokens, query_weight, query_prior, own_map, own_pool, legal_t, label)


def finish_raw(top, rest):
    rest = rest[:8] + rest[8:]
    rest = rest + jnp.concatenate([rest[4:], rest[:4]], axis=0)
    return jnp.concatenate([top, rest], axis=0)


def raw_sums(tables, pools, which):
    rows = len(pools) * pools[0].shape[2]
    total = jnp.zeros((rows, 2 * TOP * len(tables)), F32)
    lane = lax.broadcasted_iota(jnp.int32, total.shape, 1) & (2 * TOP - 1)
    for h in range(H):
        right = []
        for table in tables:
            right += [table[h * TOP : (h + 1) * TOP], table[H * TOP + h // 4 * TOP :][:TOP]]
        pooled = jnp.concatenate([pool[which, h] for pool in pools], axis=0)
        result = dot_nt(pooled, jnp.concatenate(right, axis=0))
        kept = (lane < TOP) | ((lane - TOP) >> 2 == h % 4)
        total = total + jnp.where(kept, result, 0.0)
    total = total.T
    total = sum(total[2 * TOP * i :][: 2 * TOP] for i in range(len(tables)))
    return finish_raw(total[:TOP], total[TOP:])


def lower_kernel(map_ref, own_ref, peer_ref, earlier_ref, out_ref):
    level = lax.axis_index("dp") // PAIR

    @pl.when(level == 0)
    def _():
        out_ref[...] = jnp.zeros_like(out_ref)

    @pl.when(level > 0)
    def _():
        out_ref[...] = raw_sums([map_ref[...]], [own_ref, peer_ref], 1)


def lower_raw(lower_map, own_pool, peer_pool, earlier):
    _, _, rows, half = own_pool.shape
    return pl.pallas_call(
        lower_kernel,
        in_specs=[IN_VMEM] * 4,
        out_specs=IN_VMEM,
        out_shape=jax.ShapeDtypeStruct((PAD, 2 * rows), F32),
        compiler_params=pltpu.CompilerParams(vmem_limit_bytes=12 * MIB),
        cost_estimate=pl.CostEstimate(
            flops=8 * TOP * rows * H * half, bytes_accessed=4 * rows * H * half, transcendentals=0
        ),
    )(lower_map, own_pool, peer_pool, earlier)


def policy_rows(raws, legal):
    squashed = jnp.tanh(jnp.concatenate(raws, axis=0) * (1.0 / 30.0))
    logits = 30.0 * squashed
    exp_logits = jnp.exp(logits)
    found = []
    for i in range(len(raws)):
        rows = slice(i * PAD, (i + 1) * PAD)
        weights = exp_logits[rows] * legal
        partition = jnp.sum(weights, axis=0, keepdims=True)
        found.append((squashed[rows], logits[rows], weights * (1.0 / partition), partition))
    return found


def swapped(theirs):
    rows = theirs.shape[1] // 2
    return jnp.concatenate([theirs[:, rows:], theirs[:, :rows]], axis=1)


def grad_into(out_ref, loss_ref, out_buf, loss_buf, sems, mine_ref, theirs_ref, wide_ref, turned_ref, lower):

    rows = mine_ref.shape[1] // 2
    told = jnp.concatenate([mine_ref[PAD:, :rows], theirs_ref[PAD:, :rows]], axis=1)
    move = lax.broadcasted_iota(jnp.int32, told.shape, 0)
    legal = jnp.where(move < A, told, 0.0)
    onehot = (move.astype(F32) == told[A : A + 1]).astype(F32)
    raws = [mine_ref[:PAD] + swapped(theirs_ref[:PAD])] + lower
    found = policy_rows(raws, legal)
    squashed, logits, policy, partition = found[0]
    if lower:
        partner = found[1][2]
    else:
        partner = legal * (1.0 / jnp.sum(legal, axis=0, keepdims=True))
    target = 0.5 * onehot + 0.5 * partner
    log_policy = logits - jnp.log(partition)
    loss = -jnp.sum(target * log_policy, axis=0, keepdims=True)
    loss_buf[...] = loss[:, :rows]
    loss_copy = pltpu.make_async_copy(loss_buf, loss_ref, sems.at[GRAD_CHUNKS])
    loss_copy.start()
    logit_grad = (policy - target) * (1.0 - squashed * squashed)
    high, low = split_high(logit_grad)
    left = jnp.concatenate([high.astype(F32), low.astype(F32)], axis=0).astype(BF16)
    pooled_grad = dot_tn(left, wide_ref[...]).astype(BF16)
    empty = jnp.zeros((2 * rows, DH), BF16)
    diagonal = []
    for pair in range(H // 2):
        first = pooled_grad[:, 2 * pair * DH : (2 * pair + 1) * DH]
        second = pooled_grad[:, (2 * pair + 1) * DH : 2 * (pair + 1) * DH]
        first = jnp.concatenate([first, empty], axis=1)
        second = jnp.concatenate([empty, second], axis=1)
        diagonal.append(jnp.concatenate([first, second], axis=0))
    unit = out_buf.shape[0] // GRAD_UNITS
    copies = []
    for i in range(GRAD_CHUNKS):
        part = slice(GRAD_CUTS[i] * unit, GRAD_CUTS[i + 1] * unit)
        for pair in range(H // 2):
            turned = turned_ref[part, 4 * pair * rows : 4 * (pair + 1) * rows]
            out_buf[part, 2 * pair * DH : 2 * (pair + 1) * DH] = dot_nn(turned, diagonal[pair])
        copies.append(pltpu.make_async_copy(out_buf.at[part], out_ref.at[part], sems.at[i]))
        copies[i].start()
    for copy in copies + [loss_copy]:
        copy.wait()


def lowest_grad_kernel(
    mine_ref, theirs_ref, wide_ref, turned_ref,
    out_ref, loss_ref, token_ref, out_buf, loss_buf, sems,
):
    token_ref[...] = jnp.zeros_like(token_ref)

    @pl.when(lax.axis_index("dp") // PAIR == 0)
    def _():
        grad_into(
            out_ref, loss_ref, out_buf, loss_buf, sems,
            mine_ref, theirs_ref, wide_ref, turned_ref, [],
        )


def upper_grad_kernel(
    mine_ref, theirs_ref, wide_ref, turned_ref,
    lower_ref, lower_theirs_ref, lowest_ref, lowest_loss_ref,
    out_ref, loss_ref, out_buf, loss_buf, sems,
):
    @pl.when(lax.axis_index("dp") // PAIR > 0)
    def _():
        grad_into(
            out_ref, loss_ref, out_buf, loss_buf, sems,
            mine_ref, theirs_ref, wide_ref, turned_ref,
            [lower_ref[...] + swapped(lower_theirs_ref[...])],
        )


def gradient(kernel, operands, into):
    half = operands[3].shape[0]
    rows = operands[0].shape[1] // 2
    width = H * DH
    count = len(operands)
    return pl.pallas_call(
        kernel,
        in_specs=[IN_VMEM] * count + [IN_HBM] * len(into),
        out_specs=[IN_HBM, IN_HBM] + ([] if into else [IN_VMEM]),
        out_shape=[
            jax.ShapeDtypeStruct((half, width), F32),
            jax.ShapeDtypeStruct((1, rows), F32),
        ]
        + ([] if into else [jax.ShapeDtypeStruct((8, DH), F32)]),
        input_output_aliases={count + i: i for i in range(len(into))},
        scratch_shapes=[
            pltpu.VMEM((half, width), F32),
            pltpu.VMEM((1, rows), F32),
            pltpu.SemaphoreType.DMA((GRAD_CHUNKS + 1,)),
        ],
        compiler_params=pltpu.CompilerParams(vmem_limit_bytes=16 * MIB),
        cost_estimate=pl.CostEstimate(
            flops=2 * H * PAD * half * width,
            bytes_accessed=4 * half * width + 4 * rows * H * half,
            transcendentals=0,
        ),
    )(*operands, *into)


def rotated(block, axis, distance):
    count = lax.axis_size(axis)
    return lax.ppermute(block, axis, [(i, (i + distance) % count) for i in range(count)])


def paired_device(
    tokens, legal_moves, action_label, value_weight, value_prior,
    query_weight, query_prior, policy_head, head_prior,
):
    peer_tokens = partner_2(tokens, "dp", 0)
    spread = head_spread(jnp.transpose(head_prior, (1, 0, 2)))
    prior_map = prior_fold(spread, value_prior)
    lower_map = rotated(prior_map, "dp", PAIR)
    own_pool, own_map, wide = own_side(
        tokens, query_weight, query_prior, jnp.transpose(policy_head, (1, 0, 2)), value_weight
    )
    peer_pool, mine, turned = peer_side(
        peer_tokens, query_weight, query_prior, own_map, own_pool,
        legal_moves.T, action_label.reshape(1, -1),
    )
    theirs = partner_2(mine, "dp", 0)
    operands = [mine, theirs, wide, turned]
    *lowest, token = gradient(lowest_grad_kernel, operands, [])
    lower = lower_raw(lower_map, own_pool, peer_pool, token)
    lower_theirs = partner_2(lower, "dp", 0)
    weight_grad, row_loss = gradient(upper_grad_kernel, operands + [lower, lower_theirs], lowest)
    return weight_grad, row_loss.reshape(-1)


def solution(mesh):
    paired = mesh.shape["dp"] == LEVELS * PAIR
    return jax.shard_map(
        paired_device if paired else general_device,
        mesh=mesh,
        in_specs=(
            P(("groups", "dp"), None),
            P(("groups", "dp"), None),
            P(("groups", "dp")),
            P("dp", None),
            P("dp", None),
            P(),
            P(),
            P(),
            P(),
        ),
        out_specs=(P(("groups", "dp"), None), P(("groups", "dp"))),
        check_vma=False,
    )
```
